256 devices in a mesh: ctx: 16 (over x, z_hi), tp: 16 (over y, z_lo, core).
Axes of the slice: x: 4, y: 4, z: 8 (z_hi: 4, z_lo: 2; z = z_hi * 2 + z_lo), core: 2. Of those that a mesh axis runs over, the one named last changes fastest.
Arguments:
- tokens: bfloat16 [4096, 8192], P('ctx', 'tp'), may hold values from -6 to 6
- in_weight: bfloat16 [8192, 8192], P('ctx', 'tp'), may hold values from -0.09375 to 0.09375
- filters: float32 [4096, 8192], P('ctx', 'tp'), may hold values from -1 to 1
- gate: bfloat16 [4096, 8192], P('ctx', 'tp'), may hold values from -6 to 6
- cotangent: bfloat16 [4096, 8192], P('ctx', 'tp'), may hold values from -6 to 6
Outputs:
- gated_output: bfloat16 [4096, 8192], P('ctx', 'tp')
- grad_gate: bfloat16 [4096, 8192], P('ctx', 'tp')
- grad_tokens: bfloat16 [4096, 8192], P('ctx', 'tp')
The draws below stay inside these ranges and needn't reach their ends.
All inputs are finite; a program needn't handle non-finite values.
Results may differ from the reference program's by a relative error of at most 0.028.
Values may be sent and summed in bfloat16 or wider, within the bound.
A program may use at most 128 MiB of HBM per device.

```python
import math
import jax
import jax.numpy as jnp
from jax import lax

D = 8192
LEN = 4096
CHANNELS = 512


def draw_filters(key, part):
    key = jax.random.fold_in(key, 11)
    rate_key, rough_key = jax.random.split(key)
    lowest = 8.0
    highest = 4.0 * LEN
    scales = jnp.exp(jax.random.uniform(rate_key, (D,), jnp.float32, math.log(lowest), math.log(highest)))
    rough = jnp.clip(1.5 * jax.random.normal(rough_key, (LEN, D), jnp.float32), -1.0, 1.0)
    positions = jnp.arange(LEN, dtype=jnp.float32)[:, None]
    return jnp.exp(-positions / scales) * rough * jnp.minimum(1.0, 4.0 / jnp.sqrt(scales))


def with_spikes(values, own_key, source, target, parts, factor):
    def block_of(position):
        return (jnp.arange(values.shape[position]) // (values.shape[position] // parts)).reshape((-1,) + (1,) * (values.ndim - 1 - position))

    one_side = jax.random.permutation(own_key, parts)[block_of(target)]
    other_side = (block_of(target) + parts // 2) % parts
    return jnp.where((block_of(source) == one_side) | (block_of(source) == other_side), factor * values, values)


def block_levels(stream_key, extent, cuts, low, high):
    factor_of = 1.0
    for axis_at, parts in cuts:
        heights = jax.random.uniform(jax.random.fold_in(jax.random.fold_in(stream_key, 6), axis_at), (parts,), jnp.float32, low / len(cuts), high / len(cuts))
        factor_of = factor_of * jnp.repeat(jnp.exp(heights), extent[axis_at] // parts).reshape((-1,) + (1,) * (len(extent) - 1 - axis_at))
    return factor_of


def centred(stream_key, shape, deviation, limit, shards=(), kind=jnp.bfloat16):
    values = jax.random.normal(stream_key, shape, jnp.float32) * deviation
    if len(shards) > 0:
        values = block_levels(stream_key, shape, shards, -0.22, 0.18) * values
    return jnp.clip(values, min=-limit, max=limit).astype(kind)


def bell_draw_with(key, dims, scale, reach, cuts, heavy, held_as=jnp.bfloat16):
    values = scale * jax.random.normal(key, dims, jnp.float32)
    if cuts:
        values = values * block_levels(key, dims, cuts, -0.22, 0.18)
    return jnp.clip(with_spikes(values, jax.random.fold_in(key, 3), *heavy), -reach, reach).astype(held_as)


def setup_inputs(seed: int = 0) -> dict:
    arg_keys = jax.random.split(jax.random.key(seed), 6)
    return {
        "tokens": centred(arg_keys[0], (LEN, D), 1.0, 6.0, ((0, 16), (1, 16))),
        "in_weight": bell_draw_with(arg_keys[1], (D, D), D ** -0.5, 0.09375, ((0, 16), (1, 16)), (1, 0, 16, 2.0)),
        "filters": draw_filters(jax.random.fold_in(arg_keys[5], 71), 0),
        "gate": centred(arg_keys[3], (LEN, D), 1.0, 6.0, ((0, 16), (1, 16))),
        "cotangent": centred(arg_keys[4], (LEN, D), 1.0, 6.0, ((0, 16), (1, 16))),
    }


def reference(tokens, in_weight, filters, gate, cotangent):
    values = jnp.dot(tokens, in_weight, preferred_element_type=jnp.float32).astype(jnp.bfloat16)
    gate_wide = gate.astype(jnp.float32)
    cotangent_wide = cotangent.astype(jnp.float32)
    grad_conv = cotangent_wide * gate_wide
    padded_length = 2 * LEN
    block_count = D // CHANNELS

    def channel_blocks(array):
        return array.reshape(LEN, block_count, CHANNELS).transpose(1, 0, 2)

    def merge_blocks(array):
        return array.transpose(1, 0, 2).reshape(LEN, D)

    def convolve_block(inputs):
        values_block, filter_block, grad_block = inputs
        filter_spectrum = jnp.fft.rfft(filter_block, n=padded_length, axis=0)
        forward_spectrum = jnp.fft.rfft(values_block, n=padded_length, axis=0) * filter_spectrum
        backward_spectrum = jnp.fft.rfft(grad_block, n=padded_length, axis=0) * jnp.conj(filter_spectrum)
        convolved_block = jnp.fft.irfft(forward_spectrum, n=padded_length, axis=0)[:LEN]
        backward_block = jnp.fft.irfft(backward_spectrum, n=padded_length, axis=0)[:LEN]
        return convolved_block.astype(jnp.float32), backward_block.astype(jnp.float32)

    convolved, backward = lax.map(convolve_block, (channel_blocks(values.astype(jnp.float32)), channel_blocks(filters), channel_blocks(grad_conv)))
    convolved = merge_blocks(convolved)
    backward = merge_blocks(backward)
    gated_output = (gate_wide * convolved).astype(jnp.bfloat16)
    grad_gate = (cotangent_wide * convolved).astype(jnp.bfloat16)
    grad_values = backward.astype(jnp.bfloat16)
    weight_blocks = in_weight.reshape(D, block_count, CHANNELS).transpose(1, 0, 2)

    def accumulate(running, pieces):
        grad_block, weight_block = pieces
        product_term = lax.dot_general(grad_block, weight_block, (((1,), (1,)), ((), ())), preferred_element_type=jnp.float32)
        rounded_term = lax.optimization_barrier(product_term.astype(jnp.bfloat16))
        return running + rounded_term.astype(jnp.float32), None

    starting = jnp.zeros((LEN, D), jnp.float32)
    summed, _ = lax.scan(accumulate, starting, (channel_blocks(grad_values), weight_blocks))
    return gated_output, grad_gate, summed.astype(jnp.bfloat16)
```

```python
import functools
import math

import jax
import jax.numpy as jnp
import numpy as np
from jax import lax
from jax.experimental import pallas as pl
from jax.experimental.pallas import tpu as pltpu
from jax.sharding import PartitionSpec as P

MESH = pl.DeviceIdType.MESH
F32 = jnp.float32
BF16 = jnp.bfloat16
TWO_PI = 2.0 * math.pi

XN, HN, YN = 4, 4, 4
GROUP = XN * HN
ROWS = 256
WIDE = 512
CH = WIDE // GROUP
HALF = GROUP + 1
ZROWS = HALF * CH
EXCH = 4
EROWS = WIDE // EXCH
ORDER = (0, 1, 3, 2)

A_F, A_G, A_GV, A_V, A_C = range(5)


def _add(a, b):
    if a is None:
        return b
    return a if b is None else a + b


def _sub(a, b):
    if b is None:
        return a
    return -b if a is None else a - b


def _turn(value, angle):
    re, im = value
    if re is None and im is None:
        return value
    quarter = angle / (math.pi / 2)
    if abs(quarter - round(quarter)) < 1e-9:
        q = round(quarter) % 4
        neg = lambda v: None if v is None else -v
        return [(re, im), (neg(im), re), (neg(re), neg(im)), (im, neg(re))][q]
    c, s = float(math.cos(angle)), float(math.sin(angle))
    mul = lambda v, f: None if v is None else v * f
    return _sub(mul(re, c), mul(im, s)), _add(mul(re, s), mul(im, c))


def _dft(values, sign):
    n = len(values)
    if n == 1:
        return values
    even, odd = _dft(values[0::2], sign), _dft(values[1::2], sign)
    out = [None] * n
    for k in range(n // 2):
        t = _turn(odd[k], sign * TWO_PI * k / n)
        out[k] = (_add(even[k][0], t[0]), _add(even[k][1], t[1]))
        out[k + n // 2] = (_sub(even[k][0], t[0]), _sub(even[k][1], t[1]))
    return out


def _pieces_forward(xs):
    even = _dft([(v, None) for v in xs], -1)
    odd = _dft([_turn((v, None), -TWO_PI * p / 32) for p, v in enumerate(xs)], -1)
    out = []
    for k in range(HALF):
        out.append(even[k // 2] if k % 2 == 0 else odd[k // 2])
    return out


def _pieces_inverse(zs):
    first = [(zs[0][0] * 0.5, None)] + [zs[2 * m] for m in range(1, 8)] + [(None, None)] * 8
    second = [zs[2 * m + 1] for m in range(8)] + [(None, None)] * 8
    even, odd = _dft(first, 1), _dft(second, 1)
    last = zs[16][0] * 0.5
    out = []
    for p in range(GROUP):
        turned = _turn(odd[p], TWO_PI * p / 32)[0]
        total = _add(even[p][0], turned)
        out.append(total + last if p % 2 == 0 else total - last)
    return out


def _tables():
    s = np.arange(ROWS, dtype=np.int64)
    angle = (s[:, None] * s[None, :] % ROWS) * (TWO_PI / ROWS)
    cos, sin = np.cos(angle), np.sin(angle)
    forward = np.block([[cos, -sin], [sin, cos]])
    inverse = forward.T / 4096.0
    k = np.arange(HALF)
    turn = (k[:, None] * s[None, :]) * (TWO_PI / 8192)
    twist = np.concatenate([np.cos(turn), np.sin(turn)], axis=1)
    twist = np.concatenate([twist, np.zeros((24 - HALF, 2 * ROWS))], axis=0)
    split = lambda m: np.stack([m.astype(jnp.bfloat16), (m - m.astype(jnp.bfloat16).astype(np.float64)).astype(jnp.bfloat16)])
    return split(forward), split(inverse), twist.astype(np.float32)


def _kernel(x_ref, w_ref, f_ref, gate_ref, cot_ref, fwd_ref, inv_ref, tw_ref,
            out_ref, gg_ref, gt_ref,
            wg, xg, ft, gt, fr, gr, vt, vr, gvs, gvr, cs, cr,
            zhi, zlo, spec_f, spec, vacc, dsh, dex, dsum, dy, tz, dz,
            s_a2a, r_a2a, s_w, r_w, s_e, r_e, s_w1, r_w1, s_xz, r_xz, s_xy, r_xy, s_xc, r_xc,
            s_dc, r_dc, s_dy, r_dy, s_dz, r_dz, l_w):
    i = lax.axis_index("ctx")
    j = lax.axis_index("tp")
    x, zh = i // HN, i % HN
    pair, h = zh // 2, zh % 2
    y, zl, c = j // 4, (j // 2) % 2, j % 2
    a = (c + h) % 2

    def dev(x=x, zh=zh, y=y, zl=zl, c=c):
        return (x * HN + zh, y * 4 + zl * 2 + c)

    def remote(src, dst, ssem, rsem, target):
        return pltpu.make_async_remote_copy(
            src_ref=src, dst_ref=dst, send_sem=ssem, recv_sem=rsem, device_id=target, device_id_type=MESH)

    barrier = pltpu.get_barrier_semaphore()

    def greet(target):
        pl.semaphore_signal(barrier, inc=1, device_id=target, device_id_type=MESH)

    def greet_ctx(o, carry):
        greet(((i + o) % GROUP, j))
        return carry

    lax.fori_loop(1, GROUP, greet_ctx, 0)
    for o in (1, 2, 3):
        greet(dev(y=(y + o) % YN))
    greet(dev(c=1 - c))
    greet(dev(zh=2 * pair, zl=1 - zl))
    greet(dev(zh=2 * pair + 1, zl=1 - zl))
    pl.semaphore_wait(barrier, GROUP - 1 + 3 + 1 + 2)

    def spread(kind, src_of, dst, own):
        def step(o, carry):
            g = (i + o) % GROUP
            remote(src_of(g), dst, s_a2a.at[kind, g], r_a2a.at[kind, i], (g, j)).start()
            return carry
        lax.fori_loop(1, GROUP, step, 0)
        own()

    def arrive(kind, dst_of, src):
        def step(o, carry):
            g = (i + o) % GROUP
            remote(src, dst_of(g), s_a2a.at[kind, g], r_a2a.at[kind, g], (g, j)).wait_recv()
            return carry
        lax.fori_loop(1, GROUP, step, 0)

    def sent(kind, src):
        def step(o, carry):
            g = (i + o) % GROUP
            remote(src, src, s_a2a.at[kind, g], r_a2a.at[kind, g], (g, j)).wait_send()
            return carry
        lax.fori_loop(1, GROUP, step, 0)

    def rows32(g):
        return pl.ds(pl.multiple_of(g * CH, CH), CH)

    zh_d = 2 * pair + (c + zl + pair) % 2
    t_d = (zl + pair) % 2
    myrows = pl.ds(pl.multiple_of(h * ROWS, ROWS), ROWS)
    here = zh_d == zh

    def xz_copy(which):
        target = dev(zh=zh_d, zl=zl if which == 0 else 1 - zl)
        return remote(x_ref, xg.at[t_d, y, myrows], s_xz.at[which], r_xz.at[h], target)

    xz_copy(1).start()

    @pl.when(jnp.logical_not(here))
    def _():
        xz_copy(0).start()

    @pl.when(here)
    def _():
        xg[t_d, y, myrows] = x_ref[...]

    def w_copy(o):
        return remote(w_ref, wg.at[0, x], s_w.at[o], r_w.at[x], dev(x=(x + o) % XN))

    def e_copy(k):
        part = pl.ds(k * EROWS, EROWS)
        return remote(w_ref.at[part], wg.at[1, x, part], s_e.at[k], r_e.at[k], dev(zh=3 - zh))

    w_local = pltpu.make_async_copy(w_ref, wg.at[0, x], l_w.at[0])
    w_local.start()
    for o in ORDER[1:]:
        w_copy(o).start()

    ft[...] = jnp.transpose(f_ref[...]).astype(BF16)

    def own_f():
        fr[i] = ft[rows32(i), :]

    spread(A_F, lambda g: ft.at[rows32(g)], fr.at[i], own_f)
    gt[...] = jnp.transpose(cot_ref[...].astype(F32) * gate_ref[...].astype(F32)).astype(BF16)

    def own_g():
        gr[i] = gt[rows32(i), :]

    spread(A_G, lambda g: gt.at[rows32(g)], gr.at[i], own_g)
    for k in range(EXCH):
        e_copy(k).start()

    def to_spectrum(load, out):
        def step(it, carry):
            c0 = pl.multiple_of((it // 2) * 16, 16)
            l0 = pl.multiple_of((it % 2) * 128, 128)
            zs = _pieces_forward([load(p, c0, l0) for p in range(GROUP)])
            for k in range(HALF):
                re, im = zs[k]
                if k > 0:
                    co = tw_ref[k:k + 1, pl.ds(l0, 128)]
                    si = tw_ref[k:k + 1, pl.ds(l0 + ROWS, 128)]
                    if im is None:
                        re, im = re * co, -(re * si)
                    else:
                        re, im = re * co + im * si, im * co - re * si
                if im is None:
                    im = jnp.zeros_like(re)
                at = pl.ds(pl.multiple_of(k * CH + c0, 16), 16)
                for part, off in ((re, 0), (im, ROWS)):
                    hi = part.astype(BF16)
                    zhi[at, pl.ds(l0 + off, 128)] = hi
                    zlo[at, pl.ds(l0 + off, 128)] = (part - hi.astype(F32)).astype(BF16)
            return carry
        lax.fori_loop(0, 4, step, 0)
        out[...] = (jnp.dot(zhi[...], fwd_ref[0], preferred_element_type=F32)
                    + jnp.dot(zlo[...], fwd_ref[0], preferred_element_type=F32)
                    + jnp.dot(zhi[...], fwd_ref[1], preferred_element_type=F32))

    def from_spectrum(sign, store):
        def product(k, carry):
            at = pl.ds(pl.multiple_of(k * CH, CH), CH)
            ar, ai = spec[at, :ROWS], spec[at, ROWS:]
            br, bi = spec_f[at, :ROWS], spec_f[at, ROWS:]
            if sign > 0:
                re, im = ar * br - ai * bi, ar * bi + ai * br
            else:
                re, im = ar * br + ai * bi, ai * br - ar * bi
            hr_, hi_ = re.astype(BF16), im.astype(BF16)
            zhi[at, :ROWS] = hr_
            zhi[at, ROWS:] = hi_
            zlo[at, :ROWS] = (re - hr_.astype(F32)).astype(BF16)
            zlo[at, ROWS:] = (im - hi_.astype(F32)).astype(BF16)
            return carry
        lax.fori_loop(0, HALF, product, 0)
        spec[...] = (jnp.dot(zhi[...], inv_ref[0], preferred_element_type=F32)
                     + jnp.dot(zlo[...], inv_ref[0], preferred_element_type=F32)
                     + jnp.dot(zhi[...], inv_ref[1], preferred_element_type=F32))

        def step(it, carry):
            c0 = pl.multiple_of((it // 2) * 16, 16)
            l0 = pl.multiple_of((it % 2) * 128, 128)
            zs = []
            for k in range(HALF):
                at = pl.ds(pl.multiple_of(k * CH + c0, 16), 16)
                re, im = spec[at, pl.ds(l0, 128)], spec[at, pl.ds(l0 + ROWS, 128)]
                if k > 0:
                    co = tw_ref[k:k + 1, pl.ds(l0, 128)]
                    si = tw_ref[k:k + 1, pl.ds(l0 + ROWS, 128)]
                    re, im = re * co - im * si, im * co + re * si
                zs.append((re, im))
            for p, v in enumerate(_pieces_inverse(zs)):
                store(p, c0, l0, v.astype(BF16))
            return carry
        lax.fori_loop(0, 4, step, 0)

    zl_s = (c + h + pair) % 2
    mine = jnp.logical_and(zl_s == zl, True)

    def xz_wait(hr):
        remote(x_ref, xg.at[a, y, pl.ds(hr * ROWS, ROWS)], s_xz.at[0], r_xz.at[hr], dev(c=1 - c)).wait_recv()

    for hr in (0, 1):
        @pl.when(jnp.logical_not(jnp.logical_and(hr == h, zl_s == zl)))
        def _(hr=hr):
            xz_wait(hr)

    def xy_copy(o):
        return remote(xg.at[a, y], xg.at[a, y], s_xy.at[o], r_xy.at[y], dev(y=(y + o) % YN))

    def xc_copy(yy):
        return remote(xg.at[a, yy], xg.at[a, yy], s_xc.at[yy], r_xc.at[yy], dev(c=1 - c))

    for o in ORDER[1:]:
        xy_copy(o).start()
    xc_copy(y).start()

    arrive(A_F, lambda g: fr.at[g], ft.at[rows32(0)])
    to_spectrum(lambda p, c0, l0: fr[p, pl.ds(c0, 16), pl.ds(l0, 128)].astype(F32), spec_f)
    arrive(A_G, lambda g: gr.at[g], gt.at[rows32(0)])
    to_spectrum(lambda p, c0, l0: gr[p, pl.ds(c0, 16), pl.ds(l0, 128)].astype(F32), spec)

    def store_gv(p, c0, l0, v):
        gvs[p // 2, pl.ds(c0, 16), pl.ds((p % 2) * ROWS + l0, 128)] = v

    from_spectrum(-1, store_gv)

    def own_gv():
        gvr[rows32(i), :] = gvs[i // 2]

    spread(A_GV, lambda g: gvs.at[g // 2], gvr.at[rows32(i)], own_gv)

    def w1_copy(k, o):
        part = pl.ds(k * EROWS, EROWS)
        return remote(wg.at[1, x, part], wg.at[1, x, part], s_w1.at[k, o], r_w1.at[k, x], dev(x=(x + o) % XN))

    for k in range(EXCH):
        e_copy(k).wait_recv()
        for o in ORDER[1:]:
            w1_copy(k, o).start()

    for o in ORDER[1:]:
        yy = (y + o) % YN
        remote(xg.at[a, y], xg.at[a, yy], s_xy.at[o], r_xy.at[yy], dev(c=1 - c)).wait_recv()
        xc_copy(yy).start()

    for yy in range(YN):
        remote(xg.at[a, yy], xg.at[1 - a, yy], s_xc.at[yy], r_xc.at[yy], dev(c=1 - c)).wait_recv()

    w_local.wait()

    def w_wait(o):
        xx = (x + o) % XN
        remote(w_ref, wg.at[0, xx], s_w.at[o], r_w.at[xx], dev(c=1 - c)).wait_recv()

    def w1_wait(o):
        xx = (x + o) % XN
        for k in range(EXCH):
            part = pl.ds(k * EROWS, EROWS)
            remote(w_ref.at[part], wg.at[1, xx, part], s_w1.at[k, o], r_w1.at[k, xx], dev(c=1 - c)).wait_recv()

    def value_term(t, xx, first):
        term = jnp.dot(xg[t, xx], wg[t, xx], preferred_element_type=F32)
        if first:
            vacc[...] = term
        else:
            vacc[...] += term

    def grad_term(t, xx):
        dsh[t, xx] = jnp.dot(wg[t, xx], gvr[...], preferred_element_type=F32).astype(BF16)

    def dc_copy(t, xx):
        return remote(dsh.at[t, xx], dex.at[xx], s_dc.at[xx], r_dc.at[xx], dev(c=1 - c))

    def dy_copy(yy):
        return remote(dsum.at[yy], dy.at[y], s_dy.at[yy], r_dy.at[y], dev(y=yy))

    def share(t):
        @pl.when(a != t)
        def _():
            def step(xx, carry):
                dc_copy(t, xx).start()
                return carry
            lax.fori_loop(0, XN, step, 0)

        @pl.when(a == t)
        def _():
            def step(o, carry):
                xx = (y + o) % YN
                dc_copy(t, xx).wait_recv()
                dsum[xx] = (dsh[t, xx].astype(F32) + dex[xx].astype(F32)).astype(BF16)

                @pl.when(o > 0)
                def _():
                    dy_copy(xx).start()
                return carry
            lax.fori_loop(0, YN, step, 0)

    for o in ORDER:
        if o:
            w_wait(o)
        value_term(0, (x + o) % XN, o == 0)
    arrive(A_GV, lambda g: gvr.at[rows32(g)], gvs.at[0])

    def grad_step0(xx, carry):
        grad_term(0, xx)
        return carry

    lax.fori_loop(0, XN, grad_step0, 0)
    share(0)

    for o in ORDER:
        if o:
            w1_wait(o)
        value_term(1, (x + o) % XN, False)
    vt[...] = jnp.transpose(vacc[...]).astype(BF16)
    slot = x * 2 + pair

    def own_v():
        vr[h, slot] = vt[rows32(i), :]

    spread(A_V, lambda g: vt.at[rows32(g)], vr.at[h, slot], own_v)

    def grad_step1(xx, carry):
        grad_term(1, xx)
        return carry

    lax.fori_loop(0, XN, grad_step1, 0)
    share(1)

    arrive(A_V, lambda g: vr.at[g % 2, g // 2], vt.at[rows32(0)])

    def load_v(p, c0, l0):
        at = (pl.ds(c0, 16), pl.ds((p % 2) * ROWS + l0, 128))
        return vr[0, p // 2, at[0], at[1]].astype(F32) + vr[1, p // 2, at[0], at[1]].astype(F32)

    to_spectrum(load_v, spec)

    def store_c(p, c0, l0, v):
        cs[p, pl.ds(c0, 16), pl.ds(l0, 128)] = v

    from_spectrum(1, store_c)

    def own_c():
        cr[rows32(i), :] = cs[i]

    spread(A_C, lambda g: cs.at[g], cr.at[rows32(i)], own_c)

    for o in ORDER[1:]:
        yy = (y + o) % YN
        remote(dsum.at[yy], dy.at[yy], s_dy.at[yy], r_dy.at[yy], dev(c=1 - c)).wait_recv()
    dy[y] = dsum[y]

    def dz_copy(hr):
        return remote(tz.at[hr], dz.at[zl], s_dz.at[hr], r_dz.at[zl], dev(zh=2 * pair + hr, zl=zl_s))

    for hr in (0, 1):
        cols = slice(hr * ROWS, (hr + 1) * ROWS)
        total = dy[0, :, cols].astype(F32) + dy[1, :, cols].astype(F32) + dy[2, :, cols].astype(F32) + dy[3, :, cols].astype(F32)
        tz[hr] = total.astype(BF16)
        stays = jnp.logical_and(hr == h, zl_s == zl)

        @pl.when(jnp.logical_not(stays))
        def _(hr=hr):
            dz_copy(hr).start()

        @pl.when(stays)
        def _(hr=hr):
            dz[zl] = tz[hr]

    for zz in (0, 1):
        @pl.when(jnp.logical_not(jnp.logical_and(zz == zl, here)))
        def _(zz=zz):
            remote(tz.at[0], dz.at[zz], s_dz.at[0], r_dz.at[zz], dev(c=1 - c)).wait_recv()

    gt_ref[...] = jnp.transpose(dz[0].astype(F32) + dz[1].astype(F32)).astype(BF16)

    arrive(A_C, lambda g: cr.at[rows32(g)], cs.at[0])
    conv = jnp.transpose(cr[...].astype(F32))
    out_ref[...] = (gate_ref[...].astype(F32) * conv).astype(BF16)
    gg_ref[...] = (cot_ref[...].astype(F32) * conv).astype(BF16)

    sent(A_F, ft.at[rows32(0)])
    sent(A_G, gt.at[rows32(0)])
    sent(A_GV, gvs.at[0])
    sent(A_V, vt.at[rows32(0)])
    sent(A_C, cs.at[0])
    xz_copy(1).wait_send()

    @pl.when(jnp.logical_not(here))
    def _():
        xz_copy(0).wait_send()

    for o in ORDER[1:]:
        w_copy(o).wait_send()
        xy_copy(o).wait_send()
        dy_copy((y + o) % YN).wait_send()
        for k in range(EXCH):
            w1_copy(k, o).wait_send()
    for k in range(EXCH):
        e_copy(k).wait_send()
    for q in range(4):
        xc_copy(q).wait_send()
        dc_copy(1 - a, q).wait_send()
    for hr in (0, 1):
        @pl.when(jnp.logical_not(jnp.logical_and(hr == h, zl_s == zl)))
        def _(hr=hr):
            dz_copy(hr).wait_send()


def per_device(tokens, in_weight, filters, gate, cotangent):
    forward, inverse, twist = _tables()
    vm = pltpu.VMEM
    dma = pltpu.SemaphoreType.DMA
    scratch = [
        vm((2, XN, WIDE, WIDE), BF16),
        vm((2, YN, WIDE, WIDE), BF16),
        vm((WIDE, ROWS), BF16),
        vm((WIDE, ROWS), BF16),
        vm((GROUP, CH, ROWS), BF16),
        vm((GROUP, CH, ROWS), BF16),
        vm((WIDE, WIDE), BF16),
        vm((2, GROUP // 2, CH, WIDE), BF16),
        vm((GROUP // 2, CH, WIDE), BF16),
        vm((WIDE, WIDE), BF16),
        vm((GROUP, CH, ROWS), BF16),
        vm((WIDE, ROWS), BF16),
        vm((ZROWS, WIDE), BF16),
        vm((ZROWS, WIDE), BF16),
        vm((ZROWS, WIDE), F32),
        vm((ZROWS, WIDE), F32),
        vm((WIDE, WIDE), F32),
        vm((2, XN, WIDE, WIDE), BF16),
        vm((XN, WIDE, WIDE), BF16),
        vm((YN, WIDE, WIDE), BF16),
        vm((YN, WIDE, WIDE), BF16),
        vm((2, WIDE, ROWS), BF16),
        vm((2, WIDE, ROWS), BF16),
        dma((5, GROUP)), dma((5, GROUP)),
        dma((4,)), dma((4,)),
        dma((EXCH,)), dma((EXCH,)),
        dma((EXCH, 4)), dma((EXCH, 4)),
        dma((2,)), dma((2,)),
        dma((4,)), dma((4,)),
        dma((4,)), dma((4,)),
        dma((4,)), dma((4,)),
        dma((4,)), dma((4,)),
        dma((2,)), dma((2,)),
        dma((1,)),
    ]
    block = jax.ShapeDtypeStruct((ROWS, WIDE), BF16)
    return pl.pallas_call(
        _kernel,
        out_shape=(block, block, block),
        in_specs=[pl.BlockSpec(memory_space=pltpu.VMEM)] * 8,
        out_specs=[pl.BlockSpec(memory_space=pltpu.VMEM)] * 3,
        scratch_shapes=scratch,
        compiler_params=pltpu.CompilerParams(
            collective_id=0, has_side_effects=True, vmem_limit_bytes=56 * 2**20),
        name="hyena",
    )(tokens, in_weight, filters, gate, cotangent, jnp.asarray(forward), jnp.asarray(inverse), jnp.asarray(twist))


def solution(mesh):
    placed = (P("ctx", "tp"),) * 5
    return jax.shard_map(per_device, mesh=mesh, in_specs=placed, out_specs=(P("ctx", "tp"),) * 3, check_vma=False)
```

```python
import functools
import math

import jax
import jax.numpy as jnp
import numpy as np
from jax import lax
from jax.experimental import pallas as pl
from jax.experimental.pallas import tpu as pltpu
from jax.sharding import PartitionSpec as P

MESH = pl.DeviceIdType.MESH
F32 = jnp.float32
BF16 = jnp.bfloat16
TWO_PI = 2.0 * math.pi

XN, HN, YN = 4, 4, 4
GROUP = XN * HN
ROWS = 256
WIDE = 512
CH = WIDE // GROUP
HALF = GROUP + 1
PART = CH // 2
ZROWS = HALF * PART
HW = WIDE // 2
ORDER = (0, 1, 3, 2)

A_FG, A_GV, A_V, A_C = range(4)


def _add(a, b):
    if a is None:
        return b
    return a if b is None else a + b


def _sub(a, b):
    if b is None:
        return a
    return -b if a is None else a - b


def _turn(value, angle):
    re, im = value
    if re is None and im is None:
        return value
    quarter = angle / (math.pi / 2)
    if abs(quarter - round(quarter)) < 1e-9:
        q = round(quarter) % 4
        neg = lambda v: None if v is None else -v
        return [(re, im), (neg(im), re), (neg(re), neg(im)), (im, neg(re))][q]
    c, s = float(math.cos(angle)), float(math.sin(angle))
    mul = lambda v, f: None if v is None else v * f
    return _sub(mul(re, c), mul(im, s)), _add(mul(re, s), mul(im, c))


def _dft(values, sign):
    n = len(values)
    if n == 1:
        return values
    even, odd = _dft(values[0::2], sign), _dft(values[1::2], sign)
    out = [None] * n
    for k in range(n // 2):
        t = _turn(odd[k], sign * TWO_PI * k / n)
        out[k] = (_add(even[k][0], t[0]), _add(even[k][1], t[1]))
        out[k + n // 2] = (_sub(even[k][0], t[0]), _sub(even[k][1], t[1]))
    return out


def _pieces_forward(xs):
    even = _dft([(v, None) for v in xs], -1)
    odd = _dft([_turn((v, None), -TWO_PI * p / 32) for p, v in enumerate(xs)], -1)
    out = []
    for k in range(HALF):
        out.append(even[k // 2] if k % 2 == 0 else odd[k // 2])
    return out


def _pieces_inverse(zs):
    first = [(zs[0][0] * 0.5, None)] + [zs[2 * m] for m in range(1, 8)] + [(None, None)] * 8
    second = [zs[2 * m + 1] for m in range(8)] + [(None, None)] * 8
    even, odd = _dft(first, 1), _dft(second, 1)
    last = zs[16][0] * 0.5
    out = []
    for p in range(GROUP):
        turned = _turn(odd[p], TWO_PI * p / 32)[0]
        total = _add(even[p][0], turned)
        out.append(total + last if p % 2 == 0 else total - last)
    return out


def _tables():
    s = np.arange(ROWS, dtype=np.int64)
    angle = (s[:, None] * s[None, :] % ROWS) * (TWO_PI / ROWS)
    cos, sin = np.cos(angle), np.sin(angle)
    forward = np.block([[cos, -sin], [sin, cos]])
    k = np.arange(HALF)
    turn = (k[:, None] * s[None, :]) * (TWO_PI / 8192)
    twist = np.concatenate([np.cos(turn), np.sin(turn)], axis=1)
    twist = np.concatenate([twist, np.zeros((24 - HALF, 2 * ROWS))], axis=0)
    return forward.astype(np.float32), twist.astype(np.float32)


def _kernel(x_hbm, w_hbm, f_hbm, gate_hbm, cot_hbm, dft_hbm, tw_hbm,
            conv_ref, g0_ref, g1_ref,
            x_ref, f_ref, gate_ref, cot_ref, dft_ref, tw_ref, fwd_ref, inv_ref,
            wg, xg, fg, fgr, vt, vr, gvs, gvr, cs, cr,
            zhi, zlo, spec_f, spec, vacc, dsh, dex, dsum, dy, tz, dz,
            s_a2a, r_a2a, s_gv, s_w, r_w, s_e, r_e, s_xz, r_xz, s_xy, r_xy, s_xc, r_xc,
            s_dc, r_dc, s_dy, r_dy, s_dz, r_dz, l_in):
    i = lax.axis_index("ctx")
    j = lax.axis_index("tp")
    x, zh = i // HN, i % HN
    pair, h = zh // 2, zh % 2
    y, zl, c = j // 4, (j // 2) % 2, j % 2
    a = (c + h) % 2
    pending = []

    def dev(x=x, zh=zh, y=y, zl=zl, c=c):
        return (x * HN + zh, y * 4 + zl * 2 + c)

    other = dev(c=1 - c)

    def remote(src, dst, ssem, rsem, target):
        return pltpu.make_async_remote_copy(
            src_ref=src, dst_ref=dst, send_sem=ssem, recv_sem=rsem, device_id=target, device_id_type=MESH)

    def send(copy):
        copy.start()
        pending.append(copy.wait_send)

    def send_if(cond, copy):
        pl.when(cond)(copy.start)
        pending.append(lambda: pl.when(cond)(copy.wait_send))

    loads = [pltpu.make_async_copy(src, dst, l_in.at[n]) for n, (src, dst) in enumerate((
        (f_hbm, f_ref), (gate_hbm, gate_ref), (cot_hbm, cot_ref), (x_hbm, x_ref), (w_hbm, wg.at[0, x]),
        (tw_hbm, tw_ref), (dft_hbm, dft_ref)))]
    for load in loads:
        load.start()

    barrier = pltpu.get_barrier_semaphore()

    def greet(target):
        pl.semaphore_signal(barrier, inc=1, device_id=target, device_id_type=MESH)

    def greet_ctx(o, carry):
        greet(((i + o) % GROUP, j))
        return carry

    lax.fori_loop(1, GROUP, greet_ctx, 0)
    for o in (1, 2, 3):
        greet(dev(y=(y + o) % YN))
    greet(other)
    greet(dev(zh=2 * pair, zl=1 - zl))
    greet(dev(zh=2 * pair + 1, zl=1 - zl))

    loads[0].wait()
    fg[:, :ROWS] = jnp.transpose(f_ref[...]).astype(BF16)
    loads[1].wait()
    loads[2].wait()
    fg[:, ROWS:] = jnp.transpose(cot_ref[...].astype(F32) * gate_ref[...].astype(F32)).astype(BF16)
    for load in loads[3:]:
        load.wait()
    hi = dft_ref[...].astype(BF16)
    fwd_ref[0] = hi
    fwd_ref[1] = (dft_ref[...] - hi.astype(F32)).astype(BF16)
    low, high = slice(0, ROWS), slice(ROWS, WIDE)
    for n in (0, 1):
        for rows, cols in ((low, low), (low, high), (high, low), (high, high)):
            inv_ref[n, rows, cols] = fwd_ref[n, cols, rows] * (1.0 / 4096.0)
    pl.semaphore_wait(barrier, GROUP - 1 + 3 + 1 + 2)

    def spread(kind, k, src_of, dst, own):
        def copy(o):
            g = (i + o) % GROUP
            return remote(src_of(g), dst, s_a2a.at[kind, k, g], r_a2a.at[kind, k, i], (g, j))

        def start(o, carry):
            copy(o).start()
            return carry

        def finish(o, carry):
            copy(o).wait_send()
            return carry

        lax.fori_loop(1, GROUP, start, 0)
        own()
        pending.append(lambda: lax.fori_loop(1, GROUP, finish, 0))

    def arrive(kind, k, dst_of, src):
        def step(o, carry):
            g = (i + o) % GROUP
            remote(src, dst_of(g), s_a2a.at[kind, k, g], r_a2a.at[kind, k, g], (g, j)).wait_recv()
            return carry
        lax.fori_loop(1, GROUP, step, 0)

    def chans(k, g):
        return pl.ds(pl.multiple_of(k * HW + g * PART, PART), PART)

    zh_d = 2 * pair + (c + zl + pair) % 2
    t_d = (zl + pair) % 2
    zl_s = (c + h + pair) % 2
    myrows = pl.ds(pl.multiple_of(h * ROWS, ROWS), ROWS)
    here = zh_d == zh
    stays = [jnp.logical_and(hr == h, zl_s == zl) for hr in (0, 1)]

    def xz_copy(which):
        target = dev(zh=zh_d, zl=zl if which == 0 else 1 - zl)
        return remote(x_ref, xg.at[t_d, y, myrows], s_xz.at[which], r_xz.at[h], target)

    def tokens_along_z():
        send(xz_copy(1))
        send_if(jnp.logical_not(here), xz_copy(0))

        @pl.when(here)
        def _():
            xg[t_d, y, myrows] = x_ref[...]

    def send_fg(k):
        def own():
            fgr[k, i] = fg[chans(k, i), :]

        spread(A_FG, k, lambda g: fg.at[chans(k, g)], fgr.at[k, i], own)

    right, left = dev(x=(x + 1) % XN), dev(x=(x + XN - 1) % XN)

    def block_of(o):
        return (x + o) % XN

    def piece(k, r):
        return (pl.ds(r * HW, HW), pl.ds(k * HW, HW) if k < 2 else slice(None))

    def ring(t, k, r, o, n, target):
        at = (t, block_of(o)) + piece(k, r)
        return remote(wg.at[at], wg.at[at], s_w.at[k, r, n], r_w.at[k, r, block_of(o)], target)

    def ring_wait(t, k, r, o):
        ring(t, k, r, o, 0, other).wait_recv()

    def ring_start(t, k, r):
        send(ring(t, k, r, 0, 0, right))
        send(ring(t, k, r, 0, 1, left))

    def ring_forward(t, k):
        ring_wait(t, k, 0, 3)
        send(ring(t, k, 0, 3, 2, right))
        ring_wait(t, k, 1, 1)
        send(ring(t, k, 1, 1, 2, left))

    def ring_arrive(t, k, o):
        if o in (1, 2):
            ring_wait(t, k, 0, o)
        if o in (2, 3):
            ring_wait(t, k, 1, o)

    def e_copy(k, r):
        return remote(wg.at[(0, x) + piece(k, r)], wg.at[(1, x) + piece(k, r)],
                      s_e.at[k, r], r_e.at[k, r], dev(zh=3 - zh))

    def exchange_arrive(k):
        for r in (0, 1):
            e_copy(k, r).wait_recv()
            ring_start(1, k, r)

    def to_spectrum(load, out):
        def step(it, carry):
            l0 = pl.multiple_of(it * 128, 128)
            zs = _pieces_forward([load(p, l0) for p in range(GROUP)])
            for k in range(HALF):
                re, im = zs[k]
                if k > 0:
                    co = tw_ref[k:k + 1, pl.ds(l0, 128)]
                    si = tw_ref[k:k + 1, pl.ds(l0 + ROWS, 128)]
                    if im is None:
                        re, im = re * co, -(re * si)
                    else:
                        re, im = re * co + im * si, im * co - re * si
                if im is None:
                    im = jnp.zeros_like(re)
                at = slice(k * PART, (k + 1) * PART)
                for part, off in ((re, 0), (im, ROWS)):
                    hi = part.astype(BF16)
                    zhi[at, pl.ds(l0 + off, 128)] = hi
                    zlo[at, pl.ds(l0 + off, 128)] = (part - hi.astype(F32)).astype(BF16)
            return carry
        lax.fori_loop(0, 2, step, 0)
        out[...] = (jnp.dot(zhi[...], fwd_ref[0], preferred_element_type=F32)
                    + jnp.dot(zlo[...], fwd_ref[0], preferred_element_type=F32)
                    + jnp.dot(zhi[...], fwd_ref[1], preferred_element_type=F32))

    def from_spectrum(sign, filt, store):
        def product(n, carry):
            at = pl.ds(pl.multiple_of(n * PART, PART), PART)
            ar, ai = spec[at, :ROWS], spec[at, ROWS:]
            br, bi = filt[at, :ROWS], filt[at, ROWS:]
            if sign > 0:
                re, im = ar * br - ai * bi, ar * bi + ai * br
            else:
                re, im = ar * br + ai * bi, ai * br - ar * bi
            for part, cols in ((re, slice(0, ROWS)), (im, slice(ROWS, 2 * ROWS))):
                hi = part.astype(BF16)
                zhi[at, cols] = hi
                zlo[at, cols] = (part - hi.astype(F32)).astype(BF16)
            return carry
        lax.fori_loop(0, HALF, product, 0)
        spec[...] = (jnp.dot(zhi[...], inv_ref[0], preferred_element_type=F32)
                     + jnp.dot(zlo[...], inv_ref[0], preferred_element_type=F32)
                     + jnp.dot(zhi[...], inv_ref[1], preferred_element_type=F32))

        def step(it, carry):
            l0 = pl.multiple_of(it * 128, 128)
            zs = []
            for k in range(HALF):
                at = slice(k * PART, (k + 1) * PART)
                re, im = spec[at, pl.ds(l0, 128)], spec[at, pl.ds(l0 + ROWS, 128)]
                if k > 0:
                    co = tw_ref[k:k + 1, pl.ds(l0, 128)]
                    si = tw_ref[k:k + 1, pl.ds(l0 + ROWS, 128)]
                    re, im = re * co - im * si, im * co + re * si
                zs.append((re, im))
            for p, v in enumerate(_pieces_inverse(zs)):
                store(p, l0, v.astype(BF16))
            return carry
        lax.fori_loop(0, 2, step, 0)

    up, down = dev(y=(y + 1) % YN), dev(y=(y + YN - 1) % YN)

    def xy_copy(o, hr, n, target):
        at = (a, (y + o) % YN, pl.ds(hr * ROWS, ROWS))
        return remote(xg.at[at], xg.at[at], s_xy.at[hr, n], r_xy.at[hr, (y + o) % YN], target)

    def xc_copy(yy, hr):
        at = (a, yy, pl.ds(hr * ROWS, ROWS))
        return remote(xg.at[at], xg.at[at], s_xc.at[hr, yy], r_xc.at[hr, yy], other)

    def tokens_along_y():
        for hr in (0, 1):
            wait = remote(x_ref, xg.at[a, y, pl.ds(hr * ROWS, ROWS)], s_xz.at[0], r_xz.at[hr], other).wait_recv
            pl.when(jnp.logical_not(stays[hr]))(wait)
            send(xy_copy(0, hr, 0, up))
            send(xy_copy(0, hr, 1, down))
            send(xc_copy(y, hr))

    def tokens_arrive(o, hr):
        xy_copy(o, hr, 0, other).wait_recv()
        if (o, hr) == (3, 0):
            send(xy_copy(o, hr, 2, up))
        if (o, hr) == (1, 1):
            send(xy_copy(o, hr, 2, down))
        send(xc_copy((y + o) % YN, hr))

    def tokens_from_core():
        for yy in range(YN):
            for hr in (0, 1):
                at = (1 - a, yy, pl.ds(hr * ROWS, ROWS))
                remote(xg.at[at], xg.at[at], s_xc.at[hr, yy], r_xc.at[hr, yy], other).wait_recv()

    def fg_arrive(k):
        arrive(A_FG, k, lambda g: fgr.at[k, g], fg.at[chans(k, 0)])

    def conv_grad(k):
        to_spectrum(lambda p, l0: fgr[k, p, :, pl.ds(l0, 128)].astype(F32), spec_f.at[k])
        to_spectrum(lambda p, l0: fgr[k, p, :, pl.ds(ROWS + l0, 128)].astype(F32), spec)

        def store(p, l0, v):
            gvs[k, p // 2, :, pl.ds((p % 2) * ROWS + l0, 128)] = v

        from_spectrum(-1, spec_f.at[k], store)

        for zt in (zh, 3 - zh):
            for o in range(XN):
                g = block_of(o) * HN + zt
                if o == 0 and zt is zh:
                    gvr[chans(k, i), :] = gvs[k, i // 2]
                else:
                    send(remote(gvs.at[k, g // 2], gvr.at[chans(k, i)], s_a2a.at[A_GV, k, g], r_a2a.at[A_GV, k, i], (g, j)))

    partner = 2 * pair + 1 - h

    def gv_pass(k):
        for zt in (zh, 3 - zh):
            for o in range(XN):
                g = block_of(o) * HN + zt
                at = gvr.at[chans(k, g)]
                if not (o == 0 and zt is zh):
                    remote(at, at, s_gv.at[k, g], r_a2a.at[A_GV, k, g], other).wait_recv()
                send(remote(at, at, s_gv.at[k, g], r_a2a.at[A_GV, k, g], dev(zh=partner)))

    def gv_arrive(k):
        for zt in (partner, 3 - partner):
            for o in range(XN):
                g = block_of(o) * HN + zt
                at = gvr.at[chans(k, g)]
                remote(at, at, s_gv.at[k, g], r_a2a.at[A_GV, k, g], other).wait_recv()

    def value_term(k, t, xx, first):
        term = jnp.dot(xg[t, xx], wg[t, xx, :, k * HW:(k + 1) * HW], preferred_element_type=F32)
        if first:
            vacc[k] = term
        else:
            vacc[k] += term

    def send_values(k):
        vt[k * HW:(k + 1) * HW, :] = jnp.transpose(vacc[k]).astype(BF16)
        slot = x * 2 + pair

        def own():
            vr[k, h, slot] = vt[chans(k, i), :]

        spread(A_V, k, lambda g: vt.at[chans(k, g)], vr.at[k, h, slot], own)

    def conv_forward(k):
        arrive(A_V, k, lambda g: vr.at[k, g % 2, g // 2], vt.at[chans(k, 0)])

        def load(p, l0):
            cols = pl.ds((p % 2) * ROWS + l0, 128)
            return vr[k, 0, p // 2, :, cols].astype(F32) + vr[k, 1, p // 2, :, cols].astype(F32)

        to_spectrum(load, spec)

        def store(p, l0, v):
            cs[k, p, :, pl.ds(l0, 128)] = v

        from_spectrum(1, spec_f.at[k], store)

        def own():
            cr[chans(k, i), :] = cs[k, i]

        spread(A_C, k, lambda g: cs.at[k, g], cr.at[chans(k, i)], own)

    def grad_term(t, xx):
        dsh[t, xx] = jnp.dot(wg[t, xx], gvr[...], preferred_element_type=F32).astype(BF16)

    def dc_copy(t, xx):
        return remote(dsh.at[t, xx], dex.at[xx], s_dc.at[xx], r_dc.at[xx], other)

    def dy_copy(yy, hr):
        return remote(dsum.at[yy, hr], dy.at[y, hr], s_dy.at[hr, yy], r_dy.at[hr, y], dev(y=yy))

    def grad_block(t, o):
        xx = block_of(o)
        grad_term(t, xx)
        pl.when(a != t)(dc_copy(t, xx).start)

    def grad_sum(t, o):
        xx = block_of(o)

        @pl.when(a == t)
        def _():
            dc_copy(t, xx).wait_recv()
            for hr in (0, 1):
                cols = slice(hr * ROWS, (hr + 1) * ROWS)
                dsum[xx, hr] = (dsh[t, xx, :, cols].astype(F32) + dex[xx, :, cols].astype(F32)).astype(BF16)
                pl.when(xx != y)(dy_copy(xx, hr).start)

    def dz_copy(hr):
        return remote(tz.at[hr], dz.at[zl], s_dz.at[hr], r_dz.at[zl], dev(zh=2 * pair + hr, zl=zl_s))

    def grad_along_z(hr):
        total = dsum[y, hr].astype(F32)
        for o in ORDER[1:]:
            yy = (y + o) % YN
            remote(dsum.at[yy, hr], dy.at[yy, hr], s_dy.at[hr, yy], r_dy.at[hr, yy], other).wait_recv()
        for o in ORDER[1:]:
            total += dy[(y + o) % YN, hr].astype(F32)
        tz[hr] = total.astype(BF16)
        send_if(jnp.logical_not(stays[hr]), dz_copy(hr))

        @pl.when(stays[hr])
        def _():
            dz[zl] = tz[hr]

    def grad_done():
        for zz in (0, 1):
            wait = remote(tz.at[0], dz.at[zz], s_dz.at[0], r_dz.at[zz], other).wait_recv
            pl.when(jnp.logical_not(jnp.logical_and(zz == zl, here)))(wait)
        g0_ref[...] = jnp.transpose(dz[0].astype(F32)).astype(BF16)
        g1_ref[...] = jnp.transpose(dz[1].astype(F32)).astype(BF16)

    def exchange(k):
        for r in (0, 1):
            send(e_copy(k, r))

    send_fg(0)
    send_fg(1)
    for r in (0, 1):
        ring_start(0, 2, r)
    fg_arrive(0)
    tokens_along_z()
    fg_arrive(1)
    exchange(0)
    conv_grad(0)
    ring_forward(0, 2)
    conv_grad(1)
    tokens_along_y()
    exchange_arrive(0)
    exchange(1)
    gv_pass(0)
    tokens_arrive(3, 0)
    tokens_arrive(1, 1)
    gv_pass(1)
    ring_forward(1, 0)
    exchange_arrive(1)
    tokens_arrive(1, 0)
    tokens_arrive(3, 1)
    for k in (0, 1):
        gv_arrive(k)
    for n, o in enumerate(ORDER):
        ring_arrive(0, 2, o)
        grad_block(0, o)
        if n:
            grad_sum(0, ORDER[n - 1])
    grad_sum(0, ORDER[3])
    tokens_arrive(2, 0)
    tokens_arrive(2, 1)
    ring_forward(1, 1)
    tokens_from_core()
    for o in ORDER:
        value_term(0, 0, block_of(o), o == 0)
    for o in ORDER:
        ring_arrive(1, 0, o)
        value_term(0, 1, block_of(o), False)
    send_values(0)
    for o in ORDER:
        value_term(1, 0, block_of(o), o == 0)
    for n, o in enumerate(ORDER):
        ring_arrive(1, 1, o)
        value_term(1, 1, block_of(o), False)
        if n == 3:
            send_values(1)
        grad_block(1, o)
        if n:
            grad_sum(1, ORDER[n - 1])
    grad_sum(1, ORDER[3])
    conv_forward(0)
    grad_along_z(0)
    grad_along_z(1)
    conv_forward(1)
    for k in (0, 1):
        arrive(A_C, k, lambda g: cr.at[chans(k, g)], cs.at[k, 0])
    conv_ref[...] = jnp.transpose(cr[...].astype(F32)).astype(BF16)
    grad_done()

    for wait in pending:
        wait()
    for q in range(4):
        dc_copy(1 - a, q).wait_send()
    for o in ORDER[1:]:
        for hr in (0, 1):
            dy_copy((y + o) % YN, hr).wait_send()


def per_device(tokens, in_weight, filters, gate, cotangent):
    forward, twist = _tables()
    vm = pltpu.VMEM
    dma = pltpu.SemaphoreType.DMA
    scratch = [
        vm((ROWS, WIDE), BF16),
        vm((ROWS, WIDE), F32),
        vm((ROWS, WIDE), BF16),
        vm((ROWS, WIDE), BF16),
        vm((WIDE, WIDE), F32),
        vm((24, WIDE), F32),
        vm((2, WIDE, WIDE), BF16),
        vm((2, WIDE, WIDE), BF16),
        vm((2, XN, WIDE, WIDE), BF16),
        vm((2, YN, WIDE, WIDE), BF16),
        vm((WIDE, 2 * ROWS), BF16),
        vm((2, GROUP, PART, 2 * ROWS), BF16),
        vm((WIDE, WIDE), BF16),
        vm((2, 2, GROUP // 2, PART, WIDE), BF16),
        vm((2, GROUP // 2, PART, WIDE), BF16),
        vm((WIDE, WIDE), BF16),
        vm((2, GROUP, PART, ROWS), BF16),
        vm((WIDE, ROWS), BF16),
        vm((ZROWS, WIDE), BF16),
        vm((ZROWS, WIDE), BF16),
        vm((2, ZROWS, WIDE), F32),
        vm((ZROWS, WIDE), F32),
        vm((2, WIDE, HW), F32),
        vm((2, XN, WIDE, WIDE), BF16),
        vm((XN, WIDE, WIDE), BF16),
        vm((YN, 2, WIDE, ROWS), BF16),
        vm((YN, 2, WIDE, ROWS), BF16),
        vm((2, WIDE, ROWS), BF16),
        vm((2, WIDE, ROWS), BF16),
        dma((4, 2, GROUP)), dma((4, 2, GROUP)),
        dma((2, GROUP)),
        dma((3, 2, 3)), dma((3, 2, 4)),
        dma((2, 2)), dma((2, 2)),
        dma((2,)), dma((2,)),
        dma((2, 3)), dma((2, 4)),
        dma((2, 4)), dma((2, 4)),
        dma((4,)), dma((4,)),
        dma((2, 4)), dma((2, 4)),
        dma((2,)), dma((2,)),
        dma((7,)),
    ]
    block = jax.ShapeDtypeStruct((ROWS, WIDE), BF16)
    conv, g0, g1 = pl.pallas_call(
        _kernel,
        out_shape=(block, block, block),
        in_specs=[pl.BlockSpec(memory_space=pl.ANY)] * 7,
        out_specs=[pl.BlockSpec(memory_space=pltpu.VMEM)] * 3,
        scratch_shapes=scratch,
        compiler_params=pltpu.CompilerParams(
            collective_id=0, has_side_effects=True, vmem_limit_bytes=56 * 2**20),
        name="hyena",
    )(tokens, in_weight, filters, gate, cotangent, jnp.asarray(forward), jnp.asarray(twist))
    conv = conv.astype(F32)
    gated_output = (gate.astype(F32) * conv).astype(BF16)
    grad_gate = (cotangent.astype(F32) * conv).astype(BF16)
    grad_tokens = (g0.astype(F32) + g1.astype(F32)).astype(BF16)
    return gated_output, grad_gate, grad_tokens


def solution(mesh):
    placed = (P("ctx", "tp"),) * 5
    return jax.shard_map(per_device, mesh=mesh, in_specs=placed, out_specs=(P("ctx", "tp"),) * 3, check_vma=False)
```

```python
import functools
import math

import jax
import jax.numpy as jnp
import numpy as np
from jax import lax
from jax.experimental import pallas as pl
from jax.experimental.pallas import tpu as pltpu
from jax.sharding import PartitionSpec as P

MESH = pl.DeviceIdType.MESH
F32 = jnp.float32
BF16 = jnp.bfloat16
TWO_PI = 2.0 * math.pi

XN, HN, YN = 4, 4, 4
GROUP = XN * HN
ROWS = 256
WIDE = 512
CH = WIDE // GROUP
HALF = GROUP + 1
PART = CH // 2
ZROWS = HALF * PART
HW = WIDE // 2
ORDER = (0, 1, 3, 2)
FAR_FIRST = (2, 1, 3, 0)

A_FG, A_GV, A_V, A_C = range(4)


def _add(a, b):
    if a is None:
        return b
    return a if b is None else a + b


def _sub(a, b):
    if b is None:
        return a
    return -b if a is None else a - b


def _turn(value, angle):
    re, im = value
    if re is None and im is None:
        return value
    quarter = angle / (math.pi / 2)
    if abs(quarter - round(quarter)) < 1e-9:
        q = round(quarter) % 4
        neg = lambda v: None if v is None else -v
        return [(re, im), (neg(im), re), (neg(re), neg(im)), (im, neg(re))][q]
    c, s = float(math.cos(angle)), float(math.sin(angle))
    mul = lambda v, f: None if v is None else v * f
    return _sub(mul(re, c), mul(im, s)), _add(mul(re, s), mul(im, c))


def _dft(values, sign):
    n = len(values)
    if n == 1:
        return values
    even, odd = _dft(values[0::2], sign), _dft(values[1::2], sign)
    out = [None] * n
    for k in range(n // 2):
        t = _turn(odd[k], sign * TWO_PI * k / n)
        out[k] = (_add(even[k][0], t[0]), _add(even[k][1], t[1]))
        out[k + n // 2] = (_sub(even[k][0], t[0]), _sub(even[k][1], t[1]))
    return out


def _pieces_forward(xs):
    even = _dft([(v, None) for v in xs], -1)
    odd = _dft([_turn((v, None), -TWO_PI * p / 32) for p, v in enumerate(xs)], -1)
    out = []
    for k in range(HALF):
        out.append(even[k // 2] if k % 2 == 0 else odd[k // 2])
    return out


def _pieces_inverse(zs):
    first = [(zs[0][0] * 0.5, None)] + [zs[2 * m] for m in range(1, 8)] + [(None, None)] * 8
    second = [zs[2 * m + 1] for m in range(8)] + [(None, None)] * 8
    even, odd = _dft(first, 1), _dft(second, 1)
    last = zs[16][0] * 0.5
    out = []
    for p in range(GROUP):
        turned = _turn(odd[p], TWO_PI * p / 32)[0]
        total = _add(even[p][0], turned)
        out.append(total + last if p % 2 == 0 else total - last)
    return out


def _tables():
    s = np.arange(ROWS, dtype=np.int64)
    angle = (s[:, None] * s[None, :] % ROWS) * (TWO_PI / ROWS)
    cos, sin = np.cos(angle), np.sin(angle)
    forward = np.block([[cos, -sin], [sin, cos]])
    k = np.arange(HALF)
    turn = (k[:, None] * s[None, :]) * (TWO_PI / 8192)
    twist = np.concatenate([np.cos(turn), np.sin(turn)], axis=1)
    twist = np.concatenate([twist, np.zeros((24 - HALF, 2 * ROWS))], axis=0)
    return forward.astype(np.float32), twist.astype(np.float32)


def _kernel(x_hbm, w_hbm, f_hbm, gate_hbm, cot_hbm, dft_hbm, tw_hbm,
            conv_ref, g0_ref, g1_ref,
            x_ref, f_ref, gate_ref, cot_ref, dft_ref, tw_ref, fwd_ref, inv_ref,
            wg, xg, fg, fgr, vt, vr, gvs, gvr, cs, cr,
            zs16, spec_f, spec, vacc, dsh, dex, dsum, rl, dy, tz, dz,
            s_a2a, r_a2a, s_gv, s_w, r_w, s_e, r_e, s_xz, r_xz, s_xy, r_xy, s_xc, r_xc,
            s_dc, r_dc, s_rl, r_rl, s_dy, r_dy, s_dz, r_dz, l_in):
    i = lax.axis_index("ctx")
    j = lax.axis_index("tp")
    x, zh = i // HN, i % HN
    pair, h = zh // 2, zh % 2
    y, zl, c = j // 4, (j // 2) % 2, j % 2
    a = (c + h) % 2
    pending = []

    def dev(x=x, zh=zh, y=y, zl=zl, c=c):
        return (x * HN + zh, y * 4 + zl * 2 + c)

    other = dev(c=1 - c)

    def remote(src, dst, ssem, rsem, target):
        return pltpu.make_async_remote_copy(
            src_ref=src, dst_ref=dst, send_sem=ssem, recv_sem=rsem, device_id=target, device_id_type=MESH)

    def send(copy):
        copy.start()
        pending.append(copy.wait_send)

    def send_if(cond, copy):
        pl.when(cond)(copy.start)
        pending.append(lambda: pl.when(cond)(copy.wait_send))

    loads = [pltpu.make_async_copy(src, dst, l_in.at[n]) for n, (src, dst) in enumerate((
        (f_hbm, f_ref), (gate_hbm, gate_ref), (cot_hbm, cot_ref), (x_hbm, x_ref), (w_hbm, wg.at[0, x]),
        (tw_hbm, tw_ref), (dft_hbm, dft_ref)))]
    for load in loads:
        load.start()

    barrier = pltpu.get_barrier_semaphore()

    def greet(target):
        pl.semaphore_signal(barrier, inc=1, device_id=target, device_id_type=MESH)

    def greet_ctx(o, carry):
        greet(((i + o) % GROUP, j))
        return carry

    lax.fori_loop(1, GROUP, greet_ctx, 0)
    for o in (1, 2, 3):
        greet(dev(y=(y + o) % YN))
    greet(other)
    greet(dev(zh=2 * pair, zl=1 - zl))
    greet(dev(zh=2 * pair + 1, zl=1 - zl))

    loads[0].wait()
    fg[:, :ROWS] = jnp.transpose(f_ref[...]).astype(BF16)
    loads[1].wait()
    loads[2].wait()
    fg[:, ROWS:] = jnp.transpose(cot_ref[...].astype(F32) * gate_ref[...].astype(F32)).astype(BF16)
    for load in loads[3:]:
        load.wait()
    fwd_ref[...] = dft_ref[...].astype(BF16)
    low, high = slice(0, ROWS), slice(ROWS, WIDE)
    for rows, cols in ((low, low), (low, high), (high, low), (high, high)):
        inv_ref[rows, cols] = (dft_ref[cols, rows] * (1.0 / 4096.0)).astype(BF16)
    pl.semaphore_wait(barrier, GROUP - 1 + 3 + 1 + 2)

    def spread(kind, k, src_of, dst, own):
        def copy(o):
            g = (i + o) % GROUP
            return remote(src_of(g), dst, s_a2a.at[kind, k, g], r_a2a.at[kind, k, i], (g, j))

        def start(o, carry):
            copy(o).start()
            return carry

        def finish(o, carry):
            copy(o).wait_send()
            return carry

        lax.fori_loop(1, GROUP, start, 0)
        own()
        pending.append(lambda: lax.fori_loop(1, GROUP, finish, 0))

    def arrive(kind, k, dst_of, src):
        def step(o, carry):
            g = (i + o) % GROUP
            remote(src, dst_of(g), s_a2a.at[kind, k, g], r_a2a.at[kind, k, g], (g, j)).wait_recv()
            return carry
        lax.fori_loop(1, GROUP, step, 0)

    def chans(k, g):
        return pl.ds(pl.multiple_of(k * HW + g * PART, PART), PART)

    zh_d = 2 * pair + (c + zl + pair) % 2
    t_d = (zl + pair) % 2
    zl_s = (c + h + pair) % 2
    myrows = pl.ds(pl.multiple_of(h * ROWS, ROWS), ROWS)
    here = zh_d == zh
    stays = [jnp.logical_and(hr == h, zl_s == zl) for hr in (0, 1)]

    def xz_copy(which):
        target = dev(zh=zh_d, zl=zl if which == 0 else 1 - zl)
        return remote(x_ref, xg.at[t_d, y, myrows], s_xz.at[which], r_xz.at[h], target)

    def tokens_along_z():
        send(xz_copy(1))
        send_if(jnp.logical_not(here), xz_copy(0))

        @pl.when(here)
        def _():
            xg[t_d, y, myrows] = x_ref[...]

    def send_fg(k):
        def own():
            fgr[k, i] = fg[chans(k, i), :]

        spread(A_FG, k, lambda g: fg.at[chans(k, g)], fgr.at[k, i], own)

    right, left = dev(x=(x + 1) % XN), dev(x=(x + XN - 1) % XN)

    def block_of(o):
        return (x + o) % XN

    def piece(k, r):
        return (pl.ds(r * HW, HW), pl.ds(k * HW, HW) if k < 2 else slice(None))

    def ring(t, k, r, o, n, target):
        at = (t, block_of(o)) + piece(k, r)
        return remote(wg.at[at], wg.at[at], s_w.at[k, r, n], r_w.at[k, r, block_of(o)], target)

    def ring_wait(t, k, r, o):
        ring(t, k, r, o, 0, other).wait_recv()

    def ring_start(t, k, r):
        send(ring(t, k, r, 0, 0, right))
        send(ring(t, k, r, 0, 1, left))

    def ring_forward(t, k):
        ring_wait(t, k, 0, 3)
        send(ring(t, k, 0, 3, 2, right))
        ring_wait(t, k, 1, 1)
        send(ring(t, k, 1, 1, 2, left))

    def ring_arrive(t, k, o):
        if o in (1, 2):
            ring_wait(t, k, 0, o)
        if o in (2, 3):
            ring_wait(t, k, 1, o)

    def e_copy(k, r):
        return remote(wg.at[(0, x) + piece(k, r)], wg.at[(1, x) + piece(k, r)],
                      s_e.at[k, r], r_e.at[k, r], dev(zh=3 - zh))

    def exchange_arrive(k):
        for r in (0, 1):
            e_copy(k, r).wait_recv()
            ring_start(1, k, r)

    def to_spectrum(load, out):
        def step(it, carry):
            l0 = pl.multiple_of(it * 128, 128)
            zs = _pieces_forward([load(p, l0) for p in range(GROUP)])
            for k in range(HALF):
                re, im = zs[k]
                if k > 0:
                    co = tw_ref[k:k + 1, pl.ds(l0, 128)]
                    si = tw_ref[k:k + 1, pl.ds(l0 + ROWS, 128)]
                    if im is None:
                        re, im = re * co, -(re * si)
                    else:
                        re, im = re * co + im * si, im * co - re * si
                if im is None:
                    im = jnp.zeros_like(re)
                at = slice(k * PART, (k + 1) * PART)
                zs16[at, pl.ds(l0, 128)] = re.astype(BF16)
                zs16[at, pl.ds(l0 + ROWS, 128)] = im.astype(BF16)
            return carry
        lax.fori_loop(0, 2, step, 0)
        out[...] = jnp.dot(zs16[...], fwd_ref[...], preferred_element_type=F32)

    def from_spectrum(sign, filt, store):
        def product(n, carry):
            at = pl.ds(pl.multiple_of(n * PART, PART), PART)
            ar, ai = spec[at, :ROWS], spec[at, ROWS:]
            br, bi = filt[at, :ROWS], filt[at, ROWS:]
            if sign > 0:
                re, im = ar * br - ai * bi, ar * bi + ai * br
            else:
                re, im = ar * br + ai * bi, ai * br - ar * bi
            zs16[at, :ROWS] = re.astype(BF16)
            zs16[at, ROWS:] = im.astype(BF16)
            return carry
        lax.fori_loop(0, HALF, product, 0)
        spec[...] = jnp.dot(zs16[...], inv_ref[...], preferred_element_type=F32)

        def step(it, carry):
            l0 = pl.multiple_of(it * 128, 128)
            zs = []
            for k in range(HALF):
                at = slice(k * PART, (k + 1) * PART)
                re, im = spec[at, pl.ds(l0, 128)], spec[at, pl.ds(l0 + ROWS, 128)]
                if k > 0:
                    co = tw_ref[k:k + 1, pl.ds(l0, 128)]
                    si = tw_ref[k:k + 1, pl.ds(l0 + ROWS, 128)]
                    re, im = re * co - im * si, im * co + re * si
                zs.append((re, im))
            for p, v in enumerate(_pieces_inverse(zs)):
                store(p, l0, v.astype(BF16))
            return carry
        lax.fori_loop(0, 2, step, 0)

    up, down = dev(y=(y + 1) % YN), dev(y=(y + YN - 1) % YN)

    def xy_copy(o, hr, n, target):
        at = (a, (y + o) % YN, pl.ds(hr * ROWS, ROWS))
        return remote(xg.at[at], xg.at[at], s_xy.at[hr, n], r_xy.at[hr, (y + o) % YN], target)

    def xc_copy(yy, hr):
        at = (a, yy, pl.ds(hr * ROWS, ROWS))
        return remote(xg.at[at], xg.at[at], s_xc.at[hr, yy], r_xc.at[hr, yy], other)

    def tokens_along_y():
        for hr in (0, 1):
            wait = remote(x_ref, xg.at[a, y, pl.ds(hr * ROWS, ROWS)], s_xz.at[0], r_xz.at[hr], other).wait_recv
            pl.when(jnp.logical_not(stays[hr]))(wait)
            send(xy_copy(0, hr, 0, up))
            send(xy_copy(0, hr, 1, down))
            send(xc_copy(y, hr))

    def tokens_arrive(o, hr):
        xy_copy(o, hr, 0, other).wait_recv()
        if (o, hr) == (3, 0):
            send(xy_copy(o, hr, 2, up))
        if (o, hr) == (1, 1):
            send(xy_copy(o, hr, 2, down))
        send(xc_copy((y + o) % YN, hr))

    def tokens_from_core():
        for yy in range(YN):
            for hr in (0, 1):
                at = (1 - a, yy, pl.ds(hr * ROWS, ROWS))
                remote(xg.at[at], xg.at[at], s_xc.at[hr, yy], r_xc.at[hr, yy], other).wait_recv()

    def fg_arrive(k):
        arrive(A_FG, k, lambda g: fgr.at[k, g], fg.at[chans(k, 0)])

    def conv_grad(k):
        to_spectrum(lambda p, l0: fgr[k, p, :, pl.ds(l0, 128)].astype(F32), spec_f.at[k])
        to_spectrum(lambda p, l0: fgr[k, p, :, pl.ds(ROWS + l0, 128)].astype(F32), spec)

        def store(p, l0, v):
            gvs[k, p // 2, :, pl.ds((p % 2) * ROWS + l0, 128)] = v

        from_spectrum(-1, spec_f.at[k], store)

        for zt in (zh, 3 - zh):
            for o in range(XN):
                g = block_of(o) * HN + zt
                if o == 0 and zt is zh:
                    gvr[chans(k, i), :] = gvs[k, i // 2]
                else:
                    send(remote(gvs.at[k, g // 2], gvr.at[chans(k, i)], s_a2a.at[A_GV, k, g], r_a2a.at[A_GV, k, i], (g, j)))

    partner = 2 * pair + 1 - h

    def gv_pass(k):
        for zt in (zh, 3 - zh):
            for o in range(XN):
                g = block_of(o) * HN + zt
                at = gvr.at[chans(k, g)]
                if not (o == 0 and zt is zh):
                    remote(at, at, s_gv.at[k, g], r_a2a.at[A_GV, k, g], other).wait_recv()
                send(remote(at, at, s_gv.at[k, g], r_a2a.at[A_GV, k, g], dev(zh=partner)))

    def gv_arrive(k):
        for zt in (partner, 3 - partner):
            for o in range(XN):
                g = block_of(o) * HN + zt
                at = gvr.at[chans(k, g)]
                remote(at, at, s_gv.at[k, g], r_a2a.at[A_GV, k, g], other).wait_recv()

    def value_term(k, t, xx, first):
        term = jnp.dot(xg[t, xx], wg[t, xx, :, k * HW:(k + 1) * HW], preferred_element_type=F32)
        if first:
            vacc[k] = term
        else:
            vacc[k] += term

    def send_values(k):
        vt[k * HW:(k + 1) * HW, :] = jnp.transpose(vacc[k]).astype(BF16)
        slot = x * 2 + pair

        def own():
            vr[k, h, slot] = vt[chans(k, i), :]

        spread(A_V, k, lambda g: vt.at[chans(k, g)], vr.at[k, h, slot], own)

    def conv_forward(k):
        arrive(A_V, k, lambda g: vr.at[k, g % 2, g // 2], vt.at[chans(k, 0)])

        def load(p, l0):
            cols = pl.ds((p % 2) * ROWS + l0, 128)
            return vr[k, 0, p // 2, :, cols].astype(F32) + vr[k, 1, p // 2, :, cols].astype(F32)

        to_spectrum(load, spec)

        def store(p, l0, v):
            cs[k, p, :, pl.ds(l0, 128)] = v

        from_spectrum(1, spec_f.at[k], store)

        def own():
            cr[chans(k, i), :] = cs[k, i]

        spread(A_C, k, lambda g: cs.at[k, g], cr.at[chans(k, i)], own)

    def grad_term(t, xx):
        dsh[t, xx] = jnp.dot(wg[t, xx], gvr[...], preferred_element_type=F32).astype(BF16)

    def dc_copy(t, xx):
        return remote(dsh.at[t, xx], dex.at[xx], s_dc.at[xx], r_dc.at[xx], other)

    far, above, below = (y + 2) % YN, (y + 1) % YN, (y + YN - 1) % YN

    def relay_copy(hr):
        return remote(dsum.at[far, hr], rl.at[hr], s_rl.at[hr], r_rl.at[hr], up if hr == 0 else down)

    def dy_copy(side, hr):
        yy, target = (above, up) if side == 0 else (below, down)
        return remote(dsum.at[yy, hr], dy.at[side, hr], s_dy.at[side, hr], r_dy.at[side, hr], target)

    def grad_block(t, o):
        xx = (y + o) % YN
        grad_term(t, xx)
        pl.when(a != t)(dc_copy(t, xx).start)

    def grad_sum(t, o):
        xx = (y + o) % YN

        @pl.when(a == t)
        def _():
            dc_copy(t, xx).wait_recv()
            for hr in (0, 1):
                cols = slice(hr * ROWS, (hr + 1) * ROWS)
                dsum[xx, hr] = (dsh[t, xx, :, cols].astype(F32) + dex[xx, :, cols].astype(F32)).astype(BF16)
            if o == 2:
                relay_copy(0).start()
                relay_copy(1).start()
            if o == 1:
                dy_copy(0, 1).start()
            if o == 3:
                dy_copy(1, 0).start()

    def grad_blocks(t):
        for n, o in enumerate(FAR_FIRST):
            grad_block(t, o)
            if n:
                grad_sum(t, FAR_FIRST[n - 1])
        grad_sum(t, FAR_FIRST[3])

    def grad_relay(t):
        @pl.when(a == t)
        def _():
            for hr, yy in ((0, above), (1, below)):
                relay_copy(hr).wait_recv()
                dsum[yy, hr] = (dsum[yy, hr].astype(F32) + rl[hr].astype(F32)).astype(BF16)
                dy_copy(hr, hr).start()

    def dz_copy(hr):
        return remote(tz.at[hr], dz.at[zl], s_dz.at[hr], r_dz.at[zl], dev(zh=2 * pair + hr, zl=zl_s))

    def grad_along_z(t):
        @pl.when(a == t)
        def _():
            for hr in (0, 1):
                for side in (hr, 1 - hr):
                    dy_copy(side, hr).wait_recv()
                total = dsum[y, hr].astype(F32) + dy[0, hr].astype(F32) + dy[1, hr].astype(F32)
                tz[hr] = total.astype(BF16)
                pl.when(jnp.logical_not(stays[hr]))(dz_copy(hr).start)

                @pl.when(stays[hr])
                def _(hr=hr):
                    dz[zl] = tz[hr]

    def grad_done():
        for zz in (0, 1):
            wait = remote(tz.at[0], dz.at[zz], s_dz.at[0], r_dz.at[zz], other).wait_recv
            pl.when(jnp.logical_not(jnp.logical_and(zz == zl, here)))(wait)
        g0_ref[...] = jnp.transpose(dz[0].astype(F32)).astype(BF16)
        g1_ref[...] = jnp.transpose(dz[1].astype(F32)).astype(BF16)

    def exchange(k):
        for r in (0, 1):
            send(e_copy(k, r))

    send_fg(0)
    send_fg(1)
    for r in (0, 1):
        ring_start(0, 2, r)
    fg_arrive(0)
    tokens_along_z()
    exchange(0)
    conv_grad(0)
    fg_arrive(1)
    ring_forward(0, 2)
    conv_grad(1)
    tokens_along_y()
    exchange_arrive(0)
    exchange(1)
    gv_pass(0)
    tokens_arrive(3, 0)
    tokens_arrive(1, 1)
    gv_pass(1)
    ring_forward(1, 0)
    exchange_arrive(1)
    tokens_arrive(1, 0)
    tokens_arrive(3, 1)
    for k in (0, 1):
        gv_arrive(k)
    for o in ORDER:
        ring_arrive(0, 2, o)
    grad_blocks(0)
    tokens_arrive(2, 0)
    tokens_arrive(2, 1)
    ring_forward(1, 1)
    tokens_from_core()
    for o in ORDER:
        value_term(0, 0, block_of(o), o == 0)
    for o in ORDER:
        ring_arrive(1, 0, o)
        value_term(0, 1, block_of(o), False)
    send_values(0)
    grad_relay(0)
    for o in ORDER:
        value_term(1, 0, block_of(o), o == 0)
    for o in ORDER:
        ring_arrive(1, 1, o)
    grad_blocks(1)
    for o in ORDER:
        value_term(1, 1, block_of(o), False)
    send_values(1)
    grad_along_z(0)
    grad_relay(1)
    conv_forward(0)
    grad_along_z(1)
    conv_forward(1)
    for k in (0, 1):
        arrive(A_C, k, lambda g: cr.at[chans(k, g)], cs.at[k, 0])
        cols = slice(k * HW, (k + 1) * HW)
        conv_ref[:, cols] = jnp.transpose(cr[cols, :].astype(F32)).astype(BF16)
    grad_done()

    for wait in pending:
        wait()
    for q in range(4):
        dc_copy(1 - a, q).wait_send()
    for hr in (0, 1):
        relay_copy(hr).wait_send()
        dy_copy(0, hr).wait_send()
        dy_copy(1, hr).wait_send()
        pl.when(jnp.logical_not(stays[hr]))(dz_copy(hr).wait_send)


def per_device(tokens, in_weight, filters, gate, cotangent):
    forward, twist = _tables()
    vm = pltpu.VMEM
    dma = pltpu.SemaphoreType.DMA
    scratch = [
        vm((ROWS, WIDE), BF16),
        vm((ROWS, WIDE), F32),
        vm((ROWS, WIDE), BF16),
        vm((ROWS, WIDE), BF16),
        vm((WIDE, WIDE), F32),
        vm((24, WIDE), F32),
        vm((WIDE, WIDE), BF16),
        vm((WIDE, WIDE), BF16),
        vm((2, XN, WIDE, WIDE), BF16),
        vm((2, YN, WIDE, WIDE), BF16),
        vm((WIDE, 2 * ROWS), BF16),
        vm((2, GROUP, PART, 2 * ROWS), BF16),
        vm((WIDE, WIDE), BF16),
        vm((2, 2, GROUP // 2, PART, WIDE), BF16),
        vm((2, GROUP // 2, PART, WIDE), BF16),
        vm((WIDE, WIDE), BF16),
        vm((2, GROUP, PART, ROWS), BF16),
        vm((WIDE, ROWS), BF16),
        vm((ZROWS, WIDE), BF16),
        vm((2, ZROWS, WIDE), F32),
        vm((ZROWS, WIDE), F32),
        vm((2, WIDE, HW), F32),
        vm((2, XN, WIDE, WIDE), BF16),
        vm((XN, WIDE, WIDE), BF16),
        vm((YN, 2, WIDE, ROWS), BF16),
        vm((2, WIDE, ROWS), BF16),
        vm((2, 2, WIDE, ROWS), BF16),
        vm((2, WIDE, ROWS), BF16),
        vm((2, WIDE, ROWS), BF16),
        dma((4, 2, GROUP)), dma((4, 2, GROUP)),
        dma((2, GROUP)),
        dma((3, 2, 3)), dma((3, 2, 4)),
        dma((2, 2)), dma((2, 2)),
        dma((2,)), dma((2,)),
        dma((2, 3)), dma((2, 4)),
        dma((2, 4)), dma((2, 4)),
        dma((4,)), dma((4,)),
        dma((2,)), dma((2,)),
        dma((2, 2)), dma((2, 2)),
        dma((2,)), dma((2,)),
        dma((7,)),
    ]
    block = jax.ShapeDtypeStruct((ROWS, WIDE), BF16)
    conv, g0, g1 = pl.pallas_call(
        _kernel,
        out_shape=(block, block, block),
        in_specs=[pl.BlockSpec(memory_space=pl.ANY)] * 7,
        out_specs=[pl.BlockSpec(memory_space=pltpu.VMEM)] * 3,
        scratch_shapes=scratch,
        compiler_params=pltpu.CompilerParams(
            collective_id=0, has_side_effects=True, vmem_limit_bytes=56 * 2**20),
        name="hyena",
    )(tokens, in_weight, filters, gate, cotangent, jnp.asarray(forward), jnp.asarray(twist))
    conv = conv.astype(F32)
    gated_output = (gate.astype(F32) * conv).astype(BF16)
    grad_gate = (cotangent.astype(F32) * conv).astype(BF16)
    grad_tokens = (g0.astype(F32) + g1.astype(F32)).astype(BF16)
    return gated_output, grad_gate, grad_tokens


def solution(mesh):
    placed = (P("ctx", "tp"),) * 5
    return jax.shard_map(per_device, mesh=mesh, in_specs=placed, out_specs=(P("ctx", "tp"),) * 3, check_vma=False)
```

```python
import functools
import math

import jax
import jax.numpy as jnp
import numpy as np
from jax import lax
from jax.experimental import pallas as pl
from jax.experimental.pallas import tpu as pltpu
from jax.sharding import PartitionSpec as P

MESH = pl.DeviceIdType.MESH
F32 = jnp.float32
BF16 = jnp.bfloat16
TWO_PI = 2.0 * math.pi

XN, HN, YN = 4, 4, 4
GROUP = XN * HN
ROWS = 256
WIDE = 512
CH = WIDE // GROUP
HALF = GROUP + 1
PART = CH // 2
ZROWS = HALF * PART
HW = WIDE // 2
ORDER = (0, 1, 3, 2)
FAR_FIRST = (2, 1, 3, 0)

A_FG, A_GV, A_V, A_C = range(4)


def _add(a, b):
    if a is None:
        return b
    return a if b is None else a + b


def _sub(a, b):
    if b is None:
        return a
    return -b if a is None else a - b


def _turn(value, angle):
    re, im = value
    if re is None and im is None:
        return value
    quarter = angle / (math.pi / 2)
    if abs(quarter - round(quarter)) < 1e-9:
        q = round(quarter) % 4
        neg = lambda v: None if v is None else -v
        return [(re, im), (neg(im), re), (neg(re), neg(im)), (im, neg(re))][q]
    c, s = float(math.cos(angle)), float(math.sin(angle))
    mul = lambda v, f: None if v is None else v * f
    return _sub(mul(re, c), mul(im, s)), _add(mul(re, s), mul(im, c))


def _dft(values, sign):
    n = len(values)
    if n == 1:
        return values
    even, odd = _dft(values[0::2], sign), _dft(values[1::2], sign)
    out = [None] * n
    for k in range(n // 2):
        t = _turn(odd[k], sign * TWO_PI * k / n)
        out[k] = (_add(even[k][0], t[0]), _add(even[k][1], t[1]))
        out[k + n // 2] = (_sub(even[k][0], t[0]), _sub(even[k][1], t[1]))
    return out


def _pieces_forward(xs):
    even = _dft([(v, None) for v in xs], -1)
    odd = _dft([_turn((v, None), -TWO_PI * p / 32) for p, v in enumerate(xs)], -1)
    out = []
    for k in range(HALF):
        out.append(even[k // 2] if k % 2 == 0 else odd[k // 2])
    return out


def _pieces_inverse(zs):
    first = [(zs[0][0] * 0.5, None)] + [zs[2 * m] for m in range(1, 8)] + [(None, None)] * 8
    second = [zs[2 * m + 1] for m in range(8)] + [(None, None)] * 8
    even, odd = _dft(first, 1), _dft(second, 1)
    last = zs[16][0] * 0.5
    out = []
    for p in range(GROUP):
        turned = _turn(odd[p], TWO_PI * p / 32)[0]
        total = _add(even[p][0], turned)
        out.append(total + last if p % 2 == 0 else total - last)
    return out


def _tables():
    s = np.arange(ROWS, dtype=np.int64)
    angle = (s[:, None] * s[None, :] % ROWS) * (TWO_PI / ROWS)
    cos, sin = np.cos(angle), np.sin(angle)
    forward = np.block([[cos, -sin], [sin, cos]])
    k = np.arange(HALF)
    turn = (k[:, None] * s[None, :]) * (TWO_PI / 8192)
    twist = np.concatenate([np.cos(turn), np.sin(turn)], axis=1)
    twist = np.concatenate([twist, np.zeros((24 - HALF, 2 * ROWS))], axis=0)
    return forward.astype(np.float32), twist.astype(np.float32)


def _kernel(x_hbm, w_hbm, f_hbm, gate_hbm, cot_hbm, dft_hbm, tw_hbm,
            conv_ref, g0_ref, g1_ref,
            x_ref, f_ref, gate_ref, cot_ref, dft_ref, tw_ref, fwd_ref, inv_ref,
            wg, xg, fg, fgr, vt, vr, gvs, gvr, cs, cr,
            zs16, spec_f, spec, vacc, dsh, dex, dsum, rl, dy, tz, zr, dz,
            s_a2a, r_a2a, s_gv, s_w, r_w, s_e, r_e, s_xz, r_xz, s_xy, r_xy, s_xc, r_xc,
            s_dc, r_dc, s_rl, r_rl, s_dy, r_dy, s_zr, r_zr, s_dz, r_dz, l_in):
    i = lax.axis_index("ctx")
    j = lax.axis_index("tp")
    x, zh = i // HN, i % HN
    pair, h = zh // 2, zh % 2
    y, zl, c = j // 4, (j // 2) % 2, j % 2
    a = (c + h) % 2
    pending = []

    def dev(x=x, zh=zh, y=y, zl=zl, c=c):
        return (x * HN + zh, y * 4 + zl * 2 + c)

    other = dev(c=1 - c)

    def remote(src, dst, ssem, rsem, target):
        return pltpu.make_async_remote_copy(
            src_ref=src, dst_ref=dst, send_sem=ssem, recv_sem=rsem, device_id=target, device_id_type=MESH)

    def send(copy):
        copy.start()
        pending.append(copy.wait_send)

    def send_if(cond, copy):
        pl.when(cond)(copy.start)
        pending.append(lambda: pl.when(cond)(copy.wait_send))

    loads = [pltpu.make_async_copy(src, dst, l_in.at[n]) for n, (src, dst) in enumerate((
        (f_hbm, f_ref), (gate_hbm, gate_ref), (cot_hbm, cot_ref), (x_hbm, x_ref), (w_hbm, wg.at[0, x]),
        (tw_hbm, tw_ref), (dft_hbm, dft_ref)))]
    for load in loads:
        load.start()

    barrier = pltpu.get_barrier_semaphore()

    def greet(target):
        pl.semaphore_signal(barrier, inc=1, device_id=target, device_id_type=MESH)

    def greet_ctx(o, carry):
        greet(((i + o) % GROUP, j))
        return carry

    lax.fori_loop(1, GROUP, greet_ctx, 0)
    for o in (1, 2, 3):
        greet(dev(y=(y + o) % YN))
    greet(other)
    greet(dev(zh=2 * pair, zl=1 - zl))
    greet(dev(zh=2 * pair + 1, zl=1 - zl))

    loads[0].wait()
    fg[:, :ROWS] = jnp.transpose(f_ref[...]).astype(BF16)
    loads[1].wait()
    loads[2].wait()
    fg[:, ROWS:] = jnp.transpose(cot_ref[...].astype(F32) * gate_ref[...].astype(F32)).astype(BF16)
    for load in loads[3:]:
        load.wait()
    fwd_ref[...] = dft_ref[...].astype(BF16)
    low, high = slice(0, ROWS), slice(ROWS, WIDE)
    for rows, cols in ((low, low), (low, high), (high, low), (high, high)):
        inv_ref[rows, cols] = (dft_ref[cols, rows] * (1.0 / 4096.0)).astype(BF16)
    pl.semaphore_wait(barrier, GROUP - 1 + 3 + 1 + 2)

    def spread(kind, k, src_of, dst, own):
        def copy(o):
            g = (i + o) % GROUP
            return remote(src_of(g), dst, s_a2a.at[kind, k, g], r_a2a.at[kind, k, i], (g, j))

        def start(o, carry):
            copy(o).start()
            return carry

        def finish(o, carry):
            copy(o).wait_send()
            return carry

        lax.fori_loop(1, GROUP, start, 0)
        own()
        pending.append(lambda: lax.fori_loop(1, GROUP, finish, 0))

    def arrive(kind, k, dst_of, src):
        def step(o, carry):
            g = (i + o) % GROUP
            remote(src, dst_of(g), s_a2a.at[kind, k, g], r_a2a.at[kind, k, g], (g, j)).wait_recv()
            return carry
        lax.fori_loop(1, GROUP, step, 0)

    def chans(k, g):
        return pl.ds(pl.multiple_of(k * HW + g * PART, PART), PART)

    zh_d = 2 * pair + (c + zl + pair) % 2
    t_d = (zl + pair) % 2
    zl_s = (c + h + pair) % 2
    myrows = pl.ds(pl.multiple_of(h * ROWS, ROWS), ROWS)
    here = zh_d == zh
    stays = [jnp.logical_and(hr == h, zl_s == zl) for hr in (0, 1)]

    def xz_copy(which):
        target = dev(zh=zh_d, zl=zl if which == 0 else 1 - zl)
        return remote(x_ref, xg.at[t_d, y, myrows], s_xz.at[which], r_xz.at[h], target)

    def tokens_along_z():
        send(xz_copy(1))
        send_if(jnp.logical_not(here), xz_copy(0))

        @pl.when(here)
        def _():
            xg[t_d, y, myrows] = x_ref[...]

    def send_fg(k):
        def own():
            fgr[k, i] = fg[chans(k, i), :]

        spread(A_FG, k, lambda g: fg.at[chans(k, g)], fgr.at[k, i], own)

    right, left = dev(x=(x + 1) % XN), dev(x=(x + XN - 1) % XN)

    def block_of(o):
        return (x + o) % XN

    def piece(k, r):
        return (pl.ds(r * HW, HW), pl.ds(k * HW, HW) if k < 2 else slice(None))

    def ring(t, k, r, o, n, target):
        at = (t, block_of(o)) + piece(k, r)
        return remote(wg.at[at], wg.at[at], s_w.at[k, r, n], r_w.at[k, r, block_of(o)], target)

    def ring_wait(t, k, r, o):
        ring(t, k, r, o, 0, other).wait_recv()

    def ring_start(t, k, r):
        send(ring(t, k, r, 0, 0, right))
        send(ring(t, k, r, 0, 1, left))

    def ring_forward(t, k):
        ring_wait(t, k, 0, 3)
        send(ring(t, k, 0, 3, 2, right))
        ring_wait(t, k, 1, 1)
        send(ring(t, k, 1, 1, 2, left))

    def ring_arrive(t, k, o):
        if o in (1, 2):
            ring_wait(t, k, 0, o)
        if o in (2, 3):
            ring_wait(t, k, 1, o)

    def e_copy(k, r):
        return remote(wg.at[(0, x) + piece(k, r)], wg.at[(1, x) + piece(k, r)],
                      s_e.at[k, r], r_e.at[k, r], dev(zh=3 - zh))

    def exchange_arrive(k):
        for r in (0, 1):
            e_copy(k, r).wait_recv()
            ring_start(1, k, r)

    def to_spectrum(load, out):
        def step(it, carry):
            l0 = pl.multiple_of(it * 128, 128)
            zs = _pieces_forward([load(p, l0) for p in range(GROUP)])
            for k in range(HALF):
                re, im = zs[k]
                if k > 0:
                    co = tw_ref[k:k + 1, pl.ds(l0, 128)]
                    si = tw_ref[k:k + 1, pl.ds(l0 + ROWS, 128)]
                    if im is None:
                        re, im = re * co, -(re * si)
                    else:
                        re, im = re * co + im * si, im * co - re * si
                if im is None:
                    im = jnp.zeros_like(re)
                at = slice(k * PART, (k + 1) * PART)
                zs16[at, pl.ds(l0, 128)] = re.astype(BF16)
                zs16[at, pl.ds(l0 + ROWS, 128)] = im.astype(BF16)
            return carry
        lax.fori_loop(0, 2, step, 0)
        out[...] = jnp.dot(zs16[...], fwd_ref[...], preferred_element_type=F32)

    def from_spectrum(sign, filt, store):
        def product(n, carry):
            at = pl.ds(pl.multiple_of(n * PART, PART), PART)
            ar, ai = spec[at, :ROWS], spec[at, ROWS:]
            br, bi = filt[at, :ROWS], filt[at, ROWS:]
            if sign > 0:
                re, im = ar * br - ai * bi, ar * bi + ai * br
            else:
                re, im = ar * br + ai * bi, ai * br - ar * bi
            zs16[at, :ROWS] = re.astype(BF16)
            zs16[at, ROWS:] = im.astype(BF16)
            return carry
        lax.fori_loop(0, HALF, product, 0)
        spec[...] = jnp.dot(zs16[...], inv_ref[...], preferred_element_type=F32)

        def step(it, carry):
            l0 = pl.multiple_of(it * 128, 128)
            zs = []
            for k in range(HALF):
                at = slice(k * PART, (k + 1) * PART)
                re, im = spec[at, pl.ds(l0, 128)], spec[at, pl.ds(l0 + ROWS, 128)]
                if k > 0:
                    co = tw_ref[k:k + 1, pl.ds(l0, 128)]
                    si = tw_ref[k:k + 1, pl.ds(l0 + ROWS, 128)]
                    re, im = re * co - im * si, im * co + re * si
                zs.append((re, im))
            for p, v in enumerate(_pieces_inverse(zs)):
                store(p, l0, v.astype(BF16))
            return carry
        lax.fori_loop(0, 2, step, 0)

    up, down = dev(y=(y + 1) % YN), dev(y=(y + YN - 1) % YN)

    def xy_copy(o, hr, n, target):
        at = (a, (y + o) % YN, pl.ds(hr * ROWS, ROWS))
        return remote(xg.at[at], xg.at[at], s_xy.at[hr, n], r_xy.at[hr, (y + o) % YN], target)

    def xc_copy(yy, hr):
        at = (a, yy, pl.ds(hr * ROWS, ROWS))
        return remote(xg.at[at], xg.at[at], s_xc.at[hr, yy], r_xc.at[hr, yy], other)

    def tokens_along_y():
        for hr in (0, 1):
            wait = remote(x_ref, xg.at[a, y, pl.ds(hr * ROWS, ROWS)], s_xz.at[0], r_xz.at[hr], other).wait_recv
            pl.when(jnp.logical_not(stays[hr]))(wait)
            send(xy_copy(0, hr, 0, up))
            send(xy_copy(0, hr, 1, down))
            send(xc_copy(y, hr))

    def tokens_arrive(o, hr):
        xy_copy(o, hr, 0, other).wait_recv()
        if (o, hr) == (3, 0):
            send(xy_copy(o, hr, 2, up))
        if (o, hr) == (1, 1):
            send(xy_copy(o, hr, 2, down))
        send(xc_copy((y + o) % YN, hr))

    def tokens_from_core():
        for yy in range(YN):
            for hr in (0, 1):
                at = (1 - a, yy, pl.ds(hr * ROWS, ROWS))
                remote(xg.at[at], xg.at[at], s_xc.at[hr, yy], r_xc.at[hr, yy], other).wait_recv()

    def fg_arrive(k):
        arrive(A_FG, k, lambda g: fgr.at[k, g], fg.at[chans(k, 0)])

    def conv_grad(k):
        to_spectrum(lambda p, l0: fgr[k, p, :, pl.ds(l0, 128)].astype(F32), spec_f.at[k])
        to_spectrum(lambda p, l0: fgr[k, p, :, pl.ds(ROWS + l0, 128)].astype(F32), spec)

        def store(p, l0, v):
            gvs[k, p // 2, :, pl.ds((p % 2) * ROWS + l0, 128)] = v

        from_spectrum(-1, spec_f.at[k], store)

        for zt in (zh, 3 - zh):
            for o in range(XN):
                g = block_of(o) * HN + zt
                if o == 0 and zt is zh:
                    gvr[chans(k, i), :] = gvs[k, i // 2]
                else:
                    send(remote(gvs.at[k, g // 2], gvr.at[chans(k, i)], s_a2a.at[A_GV, k, g], r_a2a.at[A_GV, k, i], (g, j)))

    partner = 2 * pair + 1 - h

    def gv_pass(k):
        for zt in (zh, 3 - zh):
            for o in range(XN):
                g = block_of(o) * HN + zt
                at = gvr.at[chans(k, g)]
                if not (o == 0 and zt is zh):
                    remote(at, at, s_gv.at[k, g], r_a2a.at[A_GV, k, g], other).wait_recv()
                send(remote(at, at, s_gv.at[k, g], r_a2a.at[A_GV, k, g], dev(zh=partner)))

    def gv_arrive(k):
        for zt in (partner, 3 - partner):
            for o in range(XN):
                g = block_of(o) * HN + zt
                at = gvr.at[chans(k, g)]
                remote(at, at, s_gv.at[k, g], r_a2a.at[A_GV, k, g], other).wait_recv()

    def value_term(k, t, xx, first):
        term = jnp.dot(xg[t, xx], wg[t, xx, :, k * HW:(k + 1) * HW], preferred_element_type=F32)
        if first:
            vacc[k] = term
        else:
            vacc[k] += term

    def send_values(k):
        vt[k * HW:(k + 1) * HW, :] = jnp.transpose(vacc[k]).astype(BF16)
        slot = x * 2 + pair

        def own():
            vr[k, h, slot] = vt[chans(k, i), :]

        spread(A_V, k, lambda g: vt.at[chans(k, g)], vr.at[k, h, slot], own)

    def conv_forward(k):
        arrive(A_V, k, lambda g: vr.at[k, g % 2, g // 2], vt.at[chans(k, 0)])

        def load(p, l0):
            cols = pl.ds((p % 2) * ROWS + l0, 128)
            return vr[k, 0, p // 2, :, cols].astype(F32) + vr[k, 1, p // 2, :, cols].astype(F32)

        to_spectrum(load, spec)

        def store(p, l0, v):
            cs[k, p, :, pl.ds(l0, 128)] = v

        from_spectrum(1, spec_f.at[k], store)

        def own():
            cr[chans(k, i), :] = cs[k, i]

        spread(A_C, k, lambda g: cs.at[k, g], cr.at[chans(k, i)], own)

    def grad_term(t, xx):
        dsh[t, xx] = jnp.dot(wg[t, xx], gvr[...], preferred_element_type=F32).astype(BF16)

    def dc_copy(t, xx):
        return remote(dsh.at[t, xx], dex.at[xx], s_dc.at[xx], r_dc.at[xx], other)

    far, above, below = (y + 2) % YN, (y + 1) % YN, (y + YN - 1) % YN

    def relay_copy(hr):
        return remote(dsum.at[far, hr], rl.at[hr], s_rl.at[hr], r_rl.at[hr], up if hr == 0 else down)

    def dy_copy(side, hr):
        yy, target = (above, up) if side == 0 else (below, down)
        return remote(dsum.at[yy, hr], dy.at[side, hr], s_dy.at[side, hr], r_dy.at[side, hr], target)

    def grad_block(t, o):
        xx = (y + o) % YN
        grad_term(t, xx)
        pl.when(a != t)(dc_copy(t, xx).start)

    def grad_sum(t, o):
        xx = (y + o) % YN

        @pl.when(a == t)
        def _():
            dc_copy(t, xx).wait_recv()
            for hr in (0, 1):
                cols = slice(hr * ROWS, (hr + 1) * ROWS)
                dsum[xx, hr] = (dsh[t, xx, :, cols].astype(F32) + dex[xx, :, cols].astype(F32)).astype(BF16)
            if o == 2:
                relay_copy(0).start()
                relay_copy(1).start()
            if o == 1:
                dy_copy(0, 1).start()
            if o == 3:
                dy_copy(1, 0).start()

    def grad_blocks(t):
        for n, o in enumerate(FAR_FIRST):
            grad_block(t, o)
            if n:
                grad_sum(t, FAR_FIRST[n - 1])
        grad_sum(t, FAR_FIRST[3])

    def grad_relay(t):
        @pl.when(a == t)
        def _():
            for hr, yy in ((0, above), (1, below)):
                relay_copy(hr).wait_recv()
                dsum[yy, hr] = (dsum[yy, hr].astype(F32) + rl[hr].astype(F32)).astype(BF16)
                dy_copy(hr, hr).start()

    cross = 1 - h
    gate_chip = zl == cross
    mate = dev(zl=1 - zl)

    def mate_copy():
        return remote(tz.at[cross], zr, s_zr.at[0], r_zr.at[0], mate)

    def near_copy():
        return remote(tz.at[h], dz.at[zl], s_dz.at[0], r_dz.at[zl], mate)

    def cross_copy():
        return remote(tz.at[cross], dz.at[0], s_dz.at[1], r_dz.at[0], dev(zh=2 * pair + cross, zl=zl_s))

    def grad_along_z(t):
        @pl.when(a == t)
        def _():
            for hr in (cross, h):
                for side in (0, 1):
                    dy_copy(side, hr).wait_recv()
                total = dsum[y, hr].astype(F32) + dy[0, hr].astype(F32) + dy[1, hr].astype(F32)
                tz[hr] = total.astype(BF16)
                if hr is cross:
                    pl.when(jnp.logical_not(gate_chip))(mate_copy().start)
                else:
                    pl.when(jnp.logical_not(here))(near_copy().start)

            @pl.when(here)
            def _():
                dz[zl] = tz[h]

    def grad_cross(t):
        @pl.when(a == t)
        def _():
            @pl.when(gate_chip)
            def _():
                mate_copy().wait_recv()
                tz[cross] = (tz[cross].astype(F32) + zr[...].astype(F32)).astype(BF16)
                cross_copy().start()

    def grad_done():
        @pl.when(here)
        def _():
            remote(tz.at[0], dz.at[1 - zl], s_dz.at[0], r_dz.at[1 - zl], other).wait_recv()

        @pl.when(jnp.logical_not(here))
        def _():
            remote(tz.at[0], dz.at[0], s_dz.at[0], r_dz.at[0], other).wait_recv()
            dz[1] = jnp.zeros((WIDE, ROWS), BF16)

        g0_ref[...] = jnp.transpose(dz[0].astype(F32)).astype(BF16)
        g1_ref[...] = jnp.transpose(dz[1].astype(F32)).astype(BF16)

    def exchange(k):
        for r in (0, 1):
            send(e_copy(k, r))

    send_fg(0)
    send_fg(1)
    for r in (0, 1):
        ring_start(0, 2, r)
    fg_arrive(0)
    tokens_along_z()
    exchange(0)
    conv_grad(0)
    fg_arrive(1)
    ring_forward(0, 2)
    conv_grad(1)
    tokens_along_y()
    exchange_arrive(0)
    exchange(1)
    gv_pass(0)
    tokens_arrive(3, 0)
    tokens_arrive(1, 1)
    gv_pass(1)
    ring_forward(1, 0)
    exchange_arrive(1)
    tokens_arrive(1, 0)
    tokens_arrive(3, 1)
    for k in (0, 1):
        gv_arrive(k)
    for o in ORDER:
        ring_arrive(0, 2, o)
    grad_blocks(0)
    tokens_arrive(2, 0)
    tokens_arrive(2, 1)
    ring_forward(1, 1)
    tokens_from_core()
    for o in ORDER:
        value_term(0, 0, block_of(o), o == 0)
    for o in ORDER:
        ring_arrive(1, 0, o)
        value_term(0, 1, block_of(o), False)
    send_values(0)
    grad_relay(0)
    for o in ORDER:
        value_term(1, 0, block_of(o), o == 0)
    for o in ORDER:
        ring_arrive(1, 1, o)
    grad_blocks(1)
    for o in ORDER:
        value_term(1, 1, block_of(o), False)
    send_values(1)
    grad_along_z(0)
    grad_relay(1)
    conv_forward(0)
    grad_cross(0)
    grad_along_z(1)
    conv_forward(1)
    grad_cross(1)
    for k in (0, 1):
        arrive(A_C, k, lambda g: cr.at[chans(k, g)], cs.at[k, 0])
        cols = slice(k * HW, (k + 1) * HW)
        conv_ref[:, cols] = jnp.transpose(cr[cols, :].astype(F32)).astype(BF16)
    grad_done()

    for wait in pending:
        wait()
    for q in range(4):
        dc_copy(1 - a, q).wait_send()
    pl.when(jnp.logical_not(here))(near_copy().wait_send)
    pl.when(jnp.logical_not(gate_chip))(mate_copy().wait_send)
    pl.when(gate_chip)(cross_copy().wait_send)
    for hr in (0, 1):
        relay_copy(hr).wait_send()
        dy_copy(0, hr).wait_send()
        dy_copy(1, hr).wait_send()


def per_device(tokens, in_weight, filters, gate, cotangent):
    forward, twist = _tables()
    vm = pltpu.VMEM
    dma = pltpu.SemaphoreType.DMA
    scratch = [
        vm((ROWS, WIDE), BF16),
        vm((ROWS, WIDE), F32),
        vm((ROWS, WIDE), BF16),
        vm((ROWS, WIDE), BF16),
        vm((WIDE, WIDE), F32),
        vm((24, WIDE), F32),
        vm((WIDE, WIDE), BF16),
        vm((WIDE, WIDE), BF16),
        vm((2, XN, WIDE, WIDE), BF16),
        vm((2, YN, WIDE, WIDE), BF16),
        vm((WIDE, 2 * ROWS), BF16),
        vm((2, GROUP, PART, 2 * ROWS), BF16),
        vm((WIDE, WIDE), BF16),
        vm((2, 2, GROUP // 2, PART, WIDE), BF16),
        vm((2, GROUP // 2, PART, WIDE), BF16),
        vm((WIDE, WIDE), BF16),
        vm((2, GROUP, PART, ROWS), BF16),
        vm((WIDE, ROWS), BF16),
        vm((ZROWS, WIDE), BF16),
        vm((2, ZROWS, WIDE), F32),
        vm((ZROWS, WIDE), F32),
        vm((2, WIDE, HW), F32),
        vm((2, XN, WIDE, WIDE), BF16),
        vm((XN, WIDE, WIDE), BF16),
        vm((YN, 2, WIDE, ROWS), BF16),
        vm((2, WIDE, ROWS), BF16),
        vm((2, 2, WIDE, ROWS), BF16),
        vm((2, WIDE, ROWS), BF16),
        vm((WIDE, ROWS), BF16),
        vm((2, WIDE, ROWS), BF16),
        dma((4, 2, GROUP)), dma((4, 2, GROUP)),
        dma((2, GROUP)),
        dma((3, 2, 3)), dma((3, 2, 4)),
        dma((2, 2)), dma((2, 2)),
        dma((2,)), dma((2,)),
        dma((2, 3)), dma((2, 4)),
        dma((2, 4)), dma((2, 4)),
        dma((4,)), dma((4,)),
        dma((2,)), dma((2,)),
        dma((2, 2)), dma((2, 2)),
        dma((1,)), dma((1,)),
        dma((2,)), dma((2,)),
        dma((7,)),
    ]
    block = jax.ShapeDtypeStruct((ROWS, WIDE), BF16)
    conv, g0, g1 = pl.pallas_call(
        _kernel,
        out_shape=(block, block, block),
        in_specs=[pl.BlockSpec(memory_space=pl.ANY)] * 7,
        out_specs=[pl.BlockSpec(memory_space=pltpu.VMEM)] * 3,
        scratch_shapes=scratch,
        compiler_params=pltpu.CompilerParams(
            collective_id=0, has_side_effects=True, vmem_limit_bytes=56 * 2**20),
        name="hyena",
    )(tokens, in_weight, filters, gate, cotangent, jnp.asarray(forward), jnp.asarray(twist))
    conv = conv.astype(F32)
    gated_output = (gate.astype(F32) * conv).astype(BF16)
    grad_gate = (cotangent.astype(F32) * conv).astype(BF16)
    grad_tokens = (g0.astype(F32) + g1.astype(F32)).astype(BF16)
    return gated_output, grad_gate, grad_tokens


def solution(mesh):
    placed = (P("ctx", "tp"),) * 5
    return jax.shard_map(per_device, mesh=mesh, in_specs=placed, out_specs=(P("ctx", "tp"),) * 3, check_vma=False)
```

```python
import functools
import math

import jax
import jax.numpy as jnp
import numpy as np
from jax import lax
from jax.experimental import pallas as pl
from jax.experimental.pallas import tpu as pltpu
from jax.sharding import PartitionSpec as P

MESH = pl.DeviceIdType.MESH
F32 = jnp.float32
BF16 = jnp.bfloat16
TWO_PI = 2.0 * math.pi

XN, HN, YN = 4, 4, 4
GROUP = XN * HN
ROWS = 256
WIDE = 512
CH = WIDE // GROUP
HALF = GROUP + 1
PART = CH // 2
ZROWS = HALF * PART
HW = WIDE // 2
ORDER = (0, 1, 3, 2)
FAR_FIRST = (2, 1, 3, 0)

A_FG, A_GV, A_V, A_C = range(4)


def _add(a, b):
    if a is None:
        return b
    return a if b is None else a + b


def _sub(a, b):
    if b is None:
        return a
    return -b if a is None else a - b


def _turn(value, angle):
    re, im = value
    if re is None and im is None:
        return value
    quarter = angle / (math.pi / 2)
    if abs(quarter - round(quarter)) < 1e-9:
        q = round(quarter) % 4
        neg = lambda v: None if v is None else -v
        return [(re, im), (neg(im), re), (neg(re), neg(im)), (im, neg(re))][q]
    c, s = float(math.cos(angle)), float(math.sin(angle))
    mul = lambda v, f: None if v is None else v * f
    return _sub(mul(re, c), mul(im, s)), _add(mul(re, s), mul(im, c))


def _dft(values, sign):
    n = len(values)
    if n == 1:
        return values
    even, odd = _dft(values[0::2], sign), _dft(values[1::2], sign)
    out = [None] * n
    for k in range(n // 2):
        t = _turn(odd[k], sign * TWO_PI * k / n)
        out[k] = (_add(even[k][0], t[0]), _add(even[k][1], t[1]))
        out[k + n // 2] = (_sub(even[k][0], t[0]), _sub(even[k][1], t[1]))
    return out


def _pieces_forward(xs):
    even = _dft([(v, None) for v in xs], -1)
    odd = _dft([_turn((v, None), -TWO_PI * p / 32) for p, v in enumerate(xs)], -1)
    out = []
    for k in range(HALF):
        out.append(even[k // 2] if k % 2 == 0 else odd[k // 2])
    return out


def _pieces_inverse(zs):
    first = [(zs[0][0] * 0.5, None)] + [zs[2 * m] for m in range(1, 8)] + [(None, None)] * 8
    second = [zs[2 * m + 1] for m in range(8)] + [(None, None)] * 8
    even, odd = _dft(first, 1), _dft(second, 1)
    last = zs[16][0] * 0.5
    out = []
    for p in range(GROUP):
        turned = _turn(odd[p], TWO_PI * p / 32)[0]
        total = _add(even[p][0], turned)
        out.append(total + last if p % 2 == 0 else total - last)
    return out


def _tables():
    s = np.arange(ROWS, dtype=np.int64)
    angle = (s[:, None] * s[None, :] % ROWS) * (TWO_PI / ROWS)
    cos, sin = np.cos(angle), np.sin(angle)
    forward = np.block([[cos, -sin], [sin, cos]])
    k = np.arange(HALF)
    turn = (k[:, None] * s[None, :]) * (TWO_PI / 8192)
    twist = np.concatenate([np.cos(turn), np.sin(turn)], axis=1)
    twist = np.concatenate([twist, np.zeros((24 - HALF, 2 * ROWS))], axis=0)
    return forward.astype(np.float32), twist.astype(np.float32)


def _kernel(x_hbm, w_hbm, f_hbm, gate_hbm, cot_hbm, dft_hbm, tw_hbm,
            conv_ref, g0_ref, g1_ref,
            x_ref, f_ref, gate_ref, cot_ref, dft_ref, tw_ref, fwd_ref, inv_ref,
            wg, xg, fg, fgr, vt, vr, gvs, gvr, cs, cr,
            zs16, spec_f, spec, vacc, dsh, dex, dsum, rl, dy, tz, zr, dz,
            s_a2a, r_a2a, s_gv, s_w, r_w, s_e, r_e, s_xz, r_xz, s_xy, r_xy, s_xc, r_xc,
            s_dc, r_dc, s_rl, r_rl, s_dy, r_dy, s_zr, r_zr, s_dz, r_dz, l_in):
    i = lax.axis_index("ctx")
    j = lax.axis_index("tp")
    x, zh = i // HN, i % HN
    pair, h = zh // 2, zh % 2
    y, zl, c = j // 4, (j // 2) % 2, j % 2
    a = (c + h) % 2
    pending = []

    def dev(x=x, zh=zh, y=y, zl=zl, c=c):
        return (x * HN + zh, y * 4 + zl * 2 + c)

    other = dev(c=1 - c)

    def remote(src, dst, ssem, rsem, target):
        return pltpu.make_async_remote_copy(
            src_ref=src, dst_ref=dst, send_sem=ssem, recv_sem=rsem, device_id=target, device_id_type=MESH)

    def send(copy):
        copy.start()
        pending.append(copy.wait_send)

    def send_if(cond, copy):
        pl.when(cond)(copy.start)
        pending.append(lambda: pl.when(cond)(copy.wait_send))

    loads = [pltpu.make_async_copy(src, dst, l_in.at[n]) for n, (src, dst) in enumerate((
        (f_hbm, f_ref), (gate_hbm, gate_ref), (cot_hbm, cot_ref), (x_hbm, x_ref), (w_hbm, wg.at[0, x]),
        (tw_hbm, tw_ref), (dft_hbm, dft_ref)))]
    for load in loads:
        load.start()

    barrier = pltpu.get_barrier_semaphore()

    def greet(target):
        pl.semaphore_signal(barrier, inc=1, device_id=target, device_id_type=MESH)

    def greet_ctx(o, carry):
        greet(((i + o) % GROUP, j))
        return carry

    lax.fori_loop(1, GROUP, greet_ctx, 0)
    for o in (1, 2, 3):
        greet(dev(y=(y + o) % YN))
    greet(other)
    greet(dev(zh=2 * pair, zl=1 - zl))
    greet(dev(zh=2 * pair + 1, zl=1 - zl))

    loads[0].wait()
    fg[:, :ROWS] = jnp.transpose(f_ref[...]).astype(BF16)
    loads[1].wait()
    loads[2].wait()
    fg[:, ROWS:] = jnp.transpose(cot_ref[...].astype(F32) * gate_ref[...].astype(F32)).astype(BF16)
    for load in loads[3:]:
        load.wait()
    fwd_ref[...] = dft_ref[...].astype(BF16)
    low, high = slice(0, ROWS), slice(ROWS, WIDE)
    for rows, cols in ((low, low), (low, high), (high, low), (high, high)):
        inv_ref[rows, cols] = (dft_ref[cols, rows] * (1.0 / 4096.0)).astype(BF16)
    pl.semaphore_wait(barrier, GROUP - 1 + 3 + 1 + 2)

    def spread(kind, k, src_of, dst, own):
        def copy(o):
            g = (i + o) % GROUP
            return remote(src_of(g), dst, s_a2a.at[kind, k, g], r_a2a.at[kind, k, i], (g, j))

        def start(o, carry):
            copy(o).start()
            return carry

        def finish(o, carry):
            copy(o).wait_send()
            return carry

        lax.fori_loop(1, GROUP, start, 0)
        own()
        pending.append(lambda: lax.fori_loop(1, GROUP, finish, 0))

    def arrive(kind, k, dst_of, src):
        def step(o, carry):
            g = (i + o) % GROUP
            remote(src, dst_of(g), s_a2a.at[kind, k, g], r_a2a.at[kind, k, g], (g, j)).wait_recv()
            return carry
        lax.fori_loop(1, GROUP, step, 0)

    def chans(k, g):
        return pl.ds(pl.multiple_of(k * HW + g * PART, PART), PART)

    zh_d = 2 * pair + (c + zl + pair) % 2
    t_d = (zl + pair) % 2
    zl_s = (c + h + pair) % 2
    myrows = pl.ds(pl.multiple_of(h * ROWS, ROWS), ROWS)
    here = zh_d == zh
    stays = [jnp.logical_and(hr == h, zl_s == zl) for hr in (0, 1)]

    def xz_copy(which):
        target = dev(zh=zh_d, zl=zl if which == 0 else 1 - zl)
        return remote(x_ref, xg.at[t_d, y, myrows], s_xz.at[which], r_xz.at[h], target)

    def tokens_along_z():
        send(xz_copy(1))
        send_if(jnp.logical_not(here), xz_copy(0))

        @pl.when(here)
        def _():
            xg[t_d, y, myrows] = x_ref[...]

    def send_fg(k):
        def own():
            fgr[k, i] = fg[chans(k, i), :]

        spread(A_FG, k, lambda g: fg.at[chans(k, g)], fgr.at[k, i], own)

    right, left = dev(x=(x + 1) % XN), dev(x=(x + XN - 1) % XN)

    def block_of(o):
        return (x + o) % XN

    def piece(k, r):
        return (pl.ds(r * HW, HW), pl.ds(k * HW, HW) if k < 2 else slice(None))

    def ring(t, k, r, o, n, target):
        at = (t, block_of(o)) + piece(k, r)
        return remote(wg.at[at], wg.at[at], s_w.at[k, r, n], r_w.at[k, r, block_of(o)], target)

    def ring_wait(t, k, r, o):
        ring(t, k, r, o, 0, other).wait_recv()

    def ring_start(t, k, r):
        send(ring(t, k, r, 0, 0, right))
        send(ring(t, k, r, 0, 1, left))

    def ring_forward(t, k):
        ring_wait(t, k, 0, 3)
        send(ring(t, k, 0, 3, 2, right))
        ring_wait(t, k, 1, 1)
        send(ring(t, k, 1, 1, 2, left))

    def ring_arrive(t, k, o):
        if o in (1, 2):
            ring_wait(t, k, 0, o)
        if o in (2, 3):
            ring_wait(t, k, 1, o)

    def e_copy(k, r):
        return remote(wg.at[(0, x) + piece(k, r)], wg.at[(1, x) + piece(k, r)],
                      s_e.at[k, r], r_e.at[k, r], dev(zh=3 - zh))

    def exchange_arrive(k):
        for r in (0, 1):
            e_copy(k, r).wait_recv()
            ring_start(1, k, r)

    def to_spectrum(load, out):
        def step(it, carry):
            l0 = pl.multiple_of(it * 128, 128)
            zs = _pieces_forward([load(p, l0) for p in range(GROUP)])
            for k in range(HALF):
                re, im = zs[k]
                if k > 0:
                    co = tw_ref[k:k + 1, pl.ds(l0, 128)]
                    si = tw_ref[k:k + 1, pl.ds(l0 + ROWS, 128)]
                    if im is None:
                        re, im = re * co, -(re * si)
                    else:
                        re, im = re * co + im * si, im * co - re * si
                if im is None:
                    im = jnp.zeros_like(re)
                at = slice(k * PART, (k + 1) * PART)
                zs16[at, pl.ds(l0, 128)] = re.astype(BF16)
                zs16[at, pl.ds(l0 + ROWS, 128)] = im.astype(BF16)
            return carry
        lax.fori_loop(0, 2, step, 0)
        out[...] = jnp.dot(zs16[...], fwd_ref[...], preferred_element_type=F32)

    def from_spectrum(sign, filt, store):
        def product(n, carry):
            at = pl.ds(pl.multiple_of(n * PART, PART), PART)
            ar, ai = spec[at, :ROWS], spec[at, ROWS:]
            br, bi = filt[at, :ROWS], filt[at, ROWS:]
            if sign > 0:
                re, im = ar * br - ai * bi, ar * bi + ai * br
            else:
                re, im = ar * br + ai * bi, ai * br - ar * bi
            zs16[at, :ROWS] = re.astype(BF16)
            zs16[at, ROWS:] = im.astype(BF16)
            return carry
        lax.fori_loop(0, HALF, product, 0)
        spec[...] = jnp.dot(zs16[...], inv_ref[...], preferred_element_type=F32)

        def step(it, carry):
            l0 = pl.multiple_of(it * 128, 128)
            zs = []
            for k in range(HALF):
                at = slice(k * PART, (k + 1) * PART)
                re, im = spec[at, pl.ds(l0, 128)], spec[at, pl.ds(l0 + ROWS, 128)]
                if k > 0:
                    co = tw_ref[k:k + 1, pl.ds(l0, 128)]
                    si = tw_ref[k:k + 1, pl.ds(l0 + ROWS, 128)]
                    re, im = re * co - im * si, im * co + re * si
                zs.append((re, im))
            for p, v in enumerate(_pieces_inverse(zs)):
                store(p, l0, v.astype(BF16))
            return carry
        lax.fori_loop(0, 2, step, 0)

    up, down = dev(y=(y + 1) % YN), dev(y=(y + YN - 1) % YN)

    def xy_copy(o, hr, n, target):
        at = (a, (y + o) % YN, pl.ds(hr * ROWS, ROWS))
        return remote(xg.at[at], xg.at[at], s_xy.at[hr, n], r_xy.at[hr, (y + o) % YN], target)

    def xc_copy(yy, hr):
        at = (a, yy, pl.ds(hr * ROWS, ROWS))
        return remote(xg.at[at], xg.at[at], s_xc.at[hr, yy], r_xc.at[hr, yy], other)

    def tokens_along_y():
        for hr in (0, 1):
            wait = remote(x_ref, xg.at[a, y, pl.ds(hr * ROWS, ROWS)], s_xz.at[0], r_xz.at[hr], other).wait_recv
            pl.when(jnp.logical_not(stays[hr]))(wait)
            send(xy_copy(0, hr, 0, up))
            send(xy_copy(0, hr, 1, down))
            send(xc_copy(y, hr))

    def tokens_arrive(o, hr):
        xy_copy(o, hr, 0, other).wait_recv()
        if (o, hr) == (3, 0):
            send(xy_copy(o, hr, 2, up))
        if (o, hr) == (1, 1):
            send(xy_copy(o, hr, 2, down))
        send(xc_copy((y + o) % YN, hr))

    def tokens_from_core():
        for yy in range(YN):
            for hr in (0, 1):
                at = (1 - a, yy, pl.ds(hr * ROWS, ROWS))
                remote(xg.at[at], xg.at[at], s_xc.at[hr, yy], r_xc.at[hr, yy], other).wait_recv()

    def fg_arrive(k):
        arrive(A_FG, k, lambda g: fgr.at[k, g], fg.at[chans(k, 0)])

    def conv_grad(k):
        to_spectrum(lambda p, l0: fgr[k, p, :, pl.ds(l0, 128)].astype(F32), spec_f.at[k])
        to_spectrum(lambda p, l0: fgr[k, p, :, pl.ds(ROWS + l0, 128)].astype(F32), spec)

        def store(p, l0, v):
            gvs[k, p // 2, :, pl.ds((p % 2) * ROWS + l0, 128)] = v

        from_spectrum(-1, spec_f.at[k], store)

        for zt in (zh, 3 - zh):
            for o in range(XN):
                g = block_of(o) * HN + zt
                if o == 0 and zt is zh:
                    gvr[chans(k, i), :] = gvs[k, i // 2]
                else:
                    send(remote(gvs.at[k, g // 2], gvr.at[chans(k, i)], s_a2a.at[A_GV, k, g], r_a2a.at[A_GV, k, i], (g, j)))

    partner = 2 * pair + 1 - h

    def gv_pass(k):
        for zt in (zh, 3 - zh):
            for o in range(XN):
                g = block_of(o) * HN + zt
                at = gvr.at[chans(k, g)]
                if not (o == 0 and zt is zh):
                    remote(at, at, s_gv.at[k, g], r_a2a.at[A_GV, k, g], other).wait_recv()
                send(remote(at, at, s_gv.at[k, g], r_a2a.at[A_GV, k, g], dev(zh=partner)))

    def gv_arrive(k):
        for zt in (partner, 3 - partner):
            for o in range(XN):
                g = block_of(o) * HN + zt
                at = gvr.at[chans(k, g)]
                remote(at, at, s_gv.at[k, g], r_a2a.at[A_GV, k, g], other).wait_recv()

    def value_term(k, t, xx, first):
        term = jnp.dot(xg[t, xx], wg[t, xx, :, k * HW:(k + 1) * HW], preferred_element_type=F32)
        if first:
            vacc[k] = term
        else:
            vacc[k] += term

    def send_values(k):
        vt[k * HW:(k + 1) * HW, :] = jnp.transpose(vacc[k]).astype(BF16)
        slot = x * 2 + pair

        def own():
            vr[k, h, slot] = vt[chans(k, i), :]

        spread(A_V, k, lambda g: vt.at[chans(k, g)], vr.at[k, h, slot], own)

    def conv_forward(k):
        arrive(A_V, k, lambda g: vr.at[k, g % 2, g // 2], vt.at[chans(k, 0)])

        def load(p, l0):
            cols = pl.ds((p % 2) * ROWS + l0, 128)
            return vr[k, 0, p // 2, :, cols].astype(F32) + vr[k, 1, p // 2, :, cols].astype(F32)

        to_spectrum(load, spec)

        def store(p, l0, v):
            cs[k, p, :, pl.ds(l0, 128)] = v

        from_spectrum(1, spec_f.at[k], store)

        def own():
            cr[chans(k, i), :] = cs[k, i]

        spread(A_C, k, lambda g: cs.at[k, g], cr.at[chans(k, i)], own)

    def grad_term(t, xx):
        dsh[t, xx] = jnp.dot(wg[t, xx], gvr[...], preferred_element_type=F32).astype(BF16)

    def dc_copy(t, xx):
        return remote(dsh.at[t, xx], dex.at[xx], s_dc.at[xx], r_dc.at[xx], other)

    far, above, below = (y + 2) % YN, (y + 1) % YN, (y + YN - 1) % YN

    def relay_copy(hr):
        return remote(dsum.at[far, hr], rl.at[hr], s_rl.at[hr], r_rl.at[hr], up if hr == 0 else down)

    def dy_copy(side, hr):
        yy, target = (above, up) if side == 0 else (below, down)
        return remote(dsum.at[yy, hr], dy.at[side, hr], s_dy.at[side, hr], r_dy.at[side, hr], target)

    def grad_block(t, o):
        xx = (y + o) % YN
        grad_term(t, xx)
        pl.when(a != t)(dc_copy(t, xx).start)

    def grad_sum(t, o):
        xx = (y + o) % YN

        @pl.when(a == t)
        def _():
            dc_copy(t, xx).wait_recv()
            for hr in (0, 1):
                cols = slice(hr * ROWS, (hr + 1) * ROWS)
                dsum[xx, hr] = (dsh[t, xx, :, cols].astype(F32) + dex[xx, :, cols].astype(F32)).astype(BF16)
            if o == 2:
                relay_copy(0).start()
                relay_copy(1).start()
            if o == 1:
                dy_copy(0, 1).start()
            if o == 3:
                dy_copy(1, 0).start()

    def grad_blocks(t):
        for n, o in enumerate(FAR_FIRST):
            grad_block(t, o)
            if n:
                grad_sum(t, FAR_FIRST[n - 1])
        grad_sum(t, FAR_FIRST[3])

    def grad_relay(t):
        @pl.when(a == t)
        def _():
            for hr, yy in ((0, above), (1, below)):
                relay_copy(hr).wait_recv()
                dsum[yy, hr] = (dsum[yy, hr].astype(F32) + rl[hr].astype(F32)).astype(BF16)
                dy_copy(hr, hr).start()

    cross = 1 - h
    gate_chip = zl == cross
    mate = dev(zl=1 - zl)

    def mate_copy():
        return remote(tz.at[cross], zr, s_zr.at[0], r_zr.at[0], mate)

    def near_copy():
        return remote(tz.at[h], dz.at[zl], s_dz.at[0], r_dz.at[zl], mate)

    def cross_copy():
        return remote(tz.at[cross], dz.at[0], s_dz.at[1], r_dz.at[0], dev(zh=2 * pair + cross, zl=zl_s))

    def grad_along_z(t):
        @pl.when(a == t)
        def _():
            for hr in (cross, h):
                for side in (0, 1):
                    dy_copy(side, hr).wait_recv()
                total = dsum[y, hr].astype(F32) + dy[0, hr].astype(F32) + dy[1, hr].astype(F32)
                tz[hr] = total.astype(BF16)
                if hr is cross:
                    pl.when(jnp.logical_not(gate_chip))(mate_copy().start)
                else:
                    pl.when(jnp.logical_not(here))(near_copy().start)

            @pl.when(here)
            def _():
                dz[zl] = tz[h]

    def grad_cross(t):
        @pl.when(a == t)
        def _():
            @pl.when(gate_chip)
            def _():
                mate_copy().wait_recv()
                tz[cross] = (tz[cross].astype(F32) + zr[...].astype(F32)).astype(BF16)
                cross_copy().start()

    def grad_done():
        @pl.when(here)
        def _():
            remote(tz.at[0], dz.at[1 - zl], s_dz.at[0], r_dz.at[1 - zl], other).wait_recv()

        @pl.when(jnp.logical_not(here))
        def _():
            remote(tz.at[0], dz.at[0], s_dz.at[0], r_dz.at[0], other).wait_recv()
            dz[1] = jnp.zeros((WIDE, ROWS), BF16)

        g0_ref[...] = jnp.transpose(dz[0].astype(F32)).astype(BF16)
        g1_ref[...] = jnp.transpose(dz[1].astype(F32)).astype(BF16)

    def exchange(k):
        for r in (0, 1):
            send(e_copy(k, r))

    send_fg(0)
    send_fg(1)
    for r in (0, 1):
        ring_start(0, 2, r)
    fg_arrive(0)
    tokens_along_z()
    exchange(0)
    conv_grad(0)
    fg_arrive(1)
    ring_forward(0, 2)
    conv_grad(1)
    tokens_along_y()
    exchange_arrive(0)
    exchange(1)
    gv_pass(0)
    tokens_arrive(3, 0)
    tokens_arrive(1, 1)
    gv_pass(1)
    ring_forward(1, 0)
    exchange_arrive(1)
    tokens_arrive(1, 0)
    tokens_arrive(3, 1)
    for k in (0, 1):
        gv_arrive(k)
    for o in ORDER:
        ring_arrive(0, 2, o)
    grad_blocks(0)
    tokens_arrive(2, 0)
    tokens_arrive(2, 1)
    ring_forward(1, 1)
    tokens_from_core()
    for o in ORDER:
        value_term(0, 0, block_of(o), o == 0)
    for o in ORDER:
        ring_arrive(1, 0, o)
        value_term(0, 1, block_of(o), False)
    send_values(0)
    grad_relay(0)
    for o in ORDER:
        value_term(1, 0, block_of(o), o == 0)
    for o in ORDER:
        ring_arrive(1, 1, o)
    grad_blocks(1)
    for o in ORDER:
        value_term(1, 1, block_of(o), False)
    send_values(1)
    grad_along_z(0)
    grad_relay(1)
    conv_forward(0)
    grad_cross(0)
    grad_along_z(1)
    conv_forward(1)
    grad_cross(1)
    for k in (0, 1):
        arrive(A_C, k, lambda g: cr.at[chans(k, g)], cs.at[k, 0])
        cols = slice(k * HW, (k + 1) * HW)
        conv_ref[:, cols] = jnp.transpose(cr[cols, :].astype(F32)).astype(BF16)
        if k == 0:
            grad_done()

    for wait in pending:
        wait()
    for q in range(4):
        dc_copy(1 - a, q).wait_send()
    pl.when(jnp.logical_not(here))(near_copy().wait_send)
    pl.when(jnp.logical_not(gate_chip))(mate_copy().wait_send)
    pl.when(gate_chip)(cross_copy().wait_send)
    for hr in (0, 1):
        relay_copy(hr).wait_send()
        dy_copy(0, hr).wait_send()
        dy_copy(1, hr).wait_send()


def per_device(tokens, in_weight, filters, gate, cotangent):
    forward, twist = _tables()
    vm = pltpu.VMEM
    dma = pltpu.SemaphoreType.DMA
    scratch = [
        vm((ROWS, WIDE), BF16),
        vm((ROWS, WIDE), F32),
        vm((ROWS, WIDE), BF16),
        vm((ROWS, WIDE), BF16),
        vm((WIDE, WIDE), F32),
        vm((24, WIDE), F32),
        vm((WIDE, WIDE), BF16),
        vm((WIDE, WIDE), BF16),
        vm((2, XN, WIDE, WIDE), BF16),
        vm((2, YN, WIDE, WIDE), BF16),
        vm((WIDE, 2 * ROWS), BF16),
        vm((2, GROUP, PART, 2 * ROWS), BF16),
        vm((WIDE, WIDE), BF16),
        vm((2, 2, GROUP // 2, PART, WIDE), BF16),
        vm((2, GROUP // 2, PART, WIDE), BF16),
        vm((WIDE, WIDE), BF16),
        vm((2, GROUP, PART, ROWS), BF16),
        vm((WIDE, ROWS), BF16),
        vm((ZROWS, WIDE), BF16),
        vm((2, ZROWS, WIDE), F32),
        vm((ZROWS, WIDE), F32),
        vm((2, WIDE, HW), F32),
        vm((2, XN, WIDE, WIDE), BF16),
        vm((XN, WIDE, WIDE), BF16),
        vm((YN, 2, WIDE, ROWS), BF16),
        vm((2, WIDE, ROWS), BF16),
        vm((2, 2, WIDE, ROWS), BF16),
        vm((2, WIDE, ROWS), BF16),
        vm((WIDE, ROWS), BF16),
        vm((2, WIDE, ROWS), BF16),
        dma((4, 2, GROUP)), dma((4, 2, GROUP)),
        dma((2, GROUP)),
        dma((3, 2, 3)), dma((3, 2, 4)),
        dma((2, 2)), dma((2, 2)),
        dma((2,)), dma((2,)),
        dma((2, 3)), dma((2, 4)),
        dma((2, 4)), dma((2, 4)),
        dma((4,)), dma((4,)),
        dma((2,)), dma((2,)),
        dma((2, 2)), dma((2, 2)),
        dma((1,)), dma((1,)),
        dma((2,)), dma((2,)),
        dma((7,)),
    ]
    block = jax.ShapeDtypeStruct((ROWS, WIDE), BF16)
    conv, g0, g1 = pl.pallas_call(
        _kernel,
        out_shape=(block, block, block),
        in_specs=[pl.BlockSpec(memory_space=pl.ANY)] * 7,
        out_specs=[pl.BlockSpec(memory_space=pltpu.VMEM)] * 3,
        scratch_shapes=scratch,
        compiler_params=pltpu.CompilerParams(
            collective_id=0, has_side_effects=True, vmem_limit_bytes=56 * 2**20),
        name="hyena",
    )(tokens, in_weight, filters, gate, cotangent, jnp.asarray(forward), jnp.asarray(twist))
    conv = conv.astype(F32)
    gated_output = (gate.astype(F32) * conv).astype(BF16)
    grad_gate = (cotangent.astype(F32) * conv).astype(BF16)
    grad_tokens = (g0.astype(F32) + g1.astype(F32)).astype(BF16)
    return gated_output, grad_gate, grad_tokens


def solution(mesh):
    placed = (P("ctx", "tp"),) * 5
    return jax.shard_map(per_device, mesh=mesh, in_specs=placed, out_specs=(P("ctx", "tp"),) * 3, check_vma=False)
```
